32 devices in a mesh: shard: 2 (over x), tm: 16 (over z, y, core).
Axes of the slice: x: 2, y: 2, z: 4, core: 2. Of those that a mesh axis runs over, the one named last changes fastest.
Arguments:
- latents: bfloat16 [128, 32, 1536], P(('shard', 'tm')), parts along dimension 0, as said below
- w_query: bfloat16 [1536, 1536], replicated, may hold values from -0.15625 to 0.15625
- w_key: bfloat16 [1536, 1536], replicated, may hold values from -0.15625 to 0.15625
- w_value: bfloat16 [1536, 1536], replicated, may hold values from -0.15625 to 0.15625
- w_out: bfloat16 [1536, 1536], replicated, may hold values from -0.15625 to 0.15625
- cotangent: bfloat16 [128, 32, 1536], P(('shard', 'tm')), parts along dimension 0, may hold values from -6 to 6
- memory_ids: int32 [128, 4], P(('shard', 'tm')), parts along dimension 0, may hold values from 0 to 63, as said below
- memory_count: int32 [128], P(('shard', 'tm')), parts along dimension 0, may hold values from 1 to 4
- tile_mask: int32 [128, 2], P(('shard', 'tm')), parts along dimension 0, may hold values 0 or 1
Outputs:
- layer_out: bfloat16 [128, 32, 1536], P(('shard', 'tm')), parts along dimension 0
- latent_grad: bfloat16 [128, 32, 1536], P(('shard', 'tm')), parts along dimension 0
The draws below stay inside these ranges and needn't reach their ends.
There are 2 independent parts, one for each index of `shard`. The reference program is written for one: setup_inputs(seed, part) draws one part's arguments, and reference() takes and returns one part's arrays. A program takes and returns all parts, laid end to end along the dimension named above; an argument that names none is the same for every part. Nothing has to cross between parts.
Inputs may be any that keep to these rules, and one draw needn't show every extreme that they name: `memory_ids`: the 16 entries of the frames of one aligned block of 4 frames (frames b * 4 to b * 4 + 3) lie in 16 different such blocks. `latents`: entries lie between -40 and 40.
All inputs are finite; a program needn't handle non-finite values. No bound on the sum of `tile_mask` on one device may be relied on, other than what follows from the above.
Results may differ from the reference program's by a relative error of at most 0.014.
The reference program's roundings to bfloat16 on the way (of `prob_low`, `mixed`, `out_grad`, `score_grad` and `query_grad`) count: a program that leaves them out, or rounds other values in their place, can miss the bound.
Values may be sent and summed in bfloat16 or wider, within the bound.
A program may use at most 192 MiB of HBM per device.

```python
import math
import jax
import jax.numpy as jnp
from jax import lax

D = 1536
HEADS = 24
TILE = 32
F_DEV = 4
MEM = 4
FRAMES = 64
INNER = 1536


def draw_latents(key, part):
    first_key = jax.random.fold_in(key, 11)
    second_key = jax.random.fold_in(key, 12)
    normal_part = jax.random.truncated_normal(first_key, -4.0, 4.0, (FRAMES, TILE, D), jnp.float32)
    low_log, high_log = (math.log(0.5), math.log(2.0))
    row_scale = jnp.exp(jax.random.uniform(second_key, (FRAMES, TILE, 1), jnp.float32, low_log, high_log))
    return (normal_part * row_scale).astype(jnp.bfloat16)


def draw_memory_ids(key, part):
    block_total = FRAMES // F_DEV

    def one_block(block_index):
        sub_key = jax.random.fold_in(jax.random.fold_in(key, 21), block_index)
        order = jax.random.permutation(jax.random.fold_in(sub_key, 1), block_total)[:F_DEV * MEM]
        offset = jax.random.randint(jax.random.fold_in(sub_key, 2), (F_DEV * MEM,), 0, F_DEV)
        return (order * F_DEV + offset).reshape(F_DEV, MEM)
    chosen = jax.vmap(one_block)(jnp.arange(block_total))
    return chosen.reshape(FRAMES, MEM).astype(jnp.int32)


def place_ends(array, stream_key, smallest, top_value):
    spot = [jax.random.randint(jax.random.fold_in(stream_key, axis), (), 0, length) for axis, length in enumerate(array.shape)]
    longest = array.shape.index(max(array.shape))
    beside = spot[:longest] + [(spot[longest] + 1) % array.shape[longest]] + spot[longest + 1:]
    return array.at[tuple(spot)].set(smallest).at[tuple(beside)].set(top_value)


def block_levels(rng, dims, split, least, high):
    def one(dim, blocks):
        heights = jax.random.uniform(jax.random.fold_in(jax.random.fold_in(rng, 6), dim), (blocks,), jnp.float32, least / len(split), high / len(split))
        return jnp.repeat(jnp.exp(heights), dims[dim] // blocks).reshape((-1,) + (1,) * (len(dims) - dim - 1))

    level = one(*split[0])
    for cut in split[1:]:
        level = level * one(*cut)
    return level


def normal_values(stream_key, dims, scale, bound, cuts=(), held_as=jnp.bfloat16):
    loudness = block_levels(stream_key, dims, cuts, -0.22, 0.18) if cuts else 1.0
    entries = jax.random.normal(stream_key, dims, jnp.float32) * scale * loudness
    return jnp.minimum(jnp.maximum(entries, -bound), bound).astype(held_as)


def setup_inputs(seed: int = 0, part: int = 0) -> dict:
    key_of = jax.random.split(jax.random.key(seed), 10)
    part_splits = jax.random.split(jax.random.fold_in(key_of[9], part), 10)
    latents = draw_latents(jax.random.fold_in(jax.random.fold_in(key_of[9], part), 71), part)
    w_query = normal_values(key_of[1], (D, INNER), D ** -0.5, 0.15625)
    w_key = normal_values(key_of[2], (D, INNER), D ** -0.5, 0.15625)
    w_value = normal_values(key_of[3], (D, INNER), D ** -0.5, 0.15625)
    w_out = normal_values(key_of[4], (INNER, D), INNER ** -0.5, 0.15625)
    cotangent = normal_values(part_splits[5], (FRAMES, TILE, D), 1.0, 6.0, ((0, 16),))
    memory_ids = draw_memory_ids(jax.random.fold_in(jax.random.fold_in(key_of[9], part), 71), part)
    memory_count = place_ends(jax.random.randint(part_splits[7], (FRAMES,), 1, MEM + 1), jax.random.fold_in(part_splits[7], 1), 1, MEM).astype(jnp.int32)
    tile_mask = place_ends((jax.random.randint(part_splits[8], (FRAMES, 2), 0, 4) < 3).astype(jnp.int32), jax.random.fold_in(part_splits[8], 1), 0, 1)
    return {"latents": latents, "w_query": w_query, "w_key": w_key, "w_value": w_value, "w_out": w_out, "cotangent": cotangent, "memory_ids": memory_ids, "memory_count": memory_count, "tile_mask": tile_mask}


def attend_forward(queries, keys, values, valid_mask):
    batch, tile_len, inner_width = queries.shape
    blocks = keys.shape[1]
    head_dim = inner_width // HEADS
    inv_root = 1.0 / math.sqrt(head_dim)
    query_four = queries.astype(jnp.float32).reshape(batch, tile_len, HEADS, head_dim)
    key_four = keys.astype(jnp.float32).reshape(batch, blocks * tile_len, HEADS, head_dim)
    value_four = values.astype(jnp.float32).reshape(batch, blocks * tile_len, HEADS, head_dim)
    scores = jnp.einsum('bqhd,bkhd->bhqk', query_four, key_four) * inv_root
    key_mask = jnp.repeat(valid_mask, tile_len, axis=1) > 0.5
    scores = jnp.where(key_mask[:, None, None, :], scores, -1e+30)
    row_max = lax.optimization_barrier(jnp.max(scores, axis=-1, keepdims=True))
    expo = jnp.exp(scores - row_max)
    attn_prob = expo / lax.optimization_barrier(jnp.sum(expo, axis=-1, keepdims=True))
    prob_low = attn_prob.astype(jnp.bfloat16)
    mixed = jnp.einsum('bhqk,bkhd->bqhd', prob_low.astype(jnp.float32), value_four)
    mixed = mixed.astype(jnp.bfloat16).reshape(batch, tile_len, inner_width)
    return (mixed, attn_prob, prob_low)

def attend_backward(queries, keys, values, attn_prob, prob_low, grad_out):
    batch, tile_len, inner_width = queries.shape
    blocks = keys.shape[1]
    head_dim = inner_width // HEADS
    inv_root = 1.0 / math.sqrt(head_dim)
    query_four = queries.astype(jnp.float32).reshape(batch, tile_len, HEADS, head_dim)
    key_four = keys.astype(jnp.float32).reshape(batch, blocks * tile_len, HEADS, head_dim)
    value_four = values.astype(jnp.float32).reshape(batch, blocks * tile_len, HEADS, head_dim)
    grad_four = grad_out.astype(jnp.float32).reshape(batch, tile_len, HEADS, head_dim)
    prob_grad = jnp.einsum('bqhd,bkhd->bhqk', grad_four, value_four)
    row_delta = lax.optimization_barrier(jnp.sum(attn_prob * prob_grad, axis=-1, keepdims=True))
    score_grad = (attn_prob * (prob_grad - row_delta) * inv_root).astype(jnp.bfloat16)
    query_grad = jnp.einsum('bhqk,bkhd->bqhd', score_grad.astype(jnp.float32), key_four)
    query_grad = query_grad.astype(jnp.bfloat16).reshape(batch, tile_len, inner_width)
    key_grad = jnp.einsum('bhqk,bqhd->bkhd', score_grad.astype(jnp.float32), query_four)
    key_grad = key_grad.astype(jnp.bfloat16).reshape(batch, blocks, tile_len, inner_width)
    value_grad = jnp.einsum('bhqk,bqhd->bkhd', prob_low.astype(jnp.float32), grad_four)
    value_grad = value_grad.astype(jnp.bfloat16).reshape(batch, blocks, tile_len, inner_width)
    return (query_grad, key_grad, value_grad)

def reference(latents, w_query, w_key, w_value, w_out, cotangent, memory_ids, memory_count, tile_mask):
    frames, tile_len, width = latents.shape
    flat_rows = latents.reshape(-1, width)

    def project(weight):
        return jnp.dot(flat_rows, weight, preferred_element_type=jnp.float32).astype(jnp.bfloat16).reshape(frames, tile_len, -1)
    queries = project(w_query)
    keys = project(w_key)
    values = project(w_value)
    inner_width = queries.shape[-1]
    out_grad = jnp.dot(cotangent.reshape(-1, width), w_out.T, preferred_element_type=jnp.float32)
    out_grad = out_grad.astype(jnp.bfloat16).reshape(frames, tile_len, inner_width)

    def frame_step(carry, index):
        key_acc, value_acc = carry
        neighbours = jnp.stack([index, index - 1, index + 1]).astype(jnp.int32)
        block_ids = jnp.concatenate([neighbours, memory_ids[index].astype(jnp.int32)])
        clipped = jnp.clip(block_ids, 0, frames - 1).astype(jnp.int32)
        lower = (tile_mask[index, 0] * (index >= 1)).astype(jnp.float32)
        upper = (tile_mask[index, 1] * (index < frames - 1)).astype(jnp.float32)
        remembered = (jnp.arange(MEM) < memory_count[index]).astype(jnp.float32)
        valid_mask = jnp.concatenate([jnp.ones((1,), jnp.float32), lower[None], upper[None], remembered])
        key_blocks = keys[clipped]
        value_blocks = values[clipped]
        mixed, attn_prob, prob_low = attend_forward(queries[index][None], key_blocks[None], value_blocks[None], valid_mask[None])
        query_grad, key_grad, value_grad = attend_backward(queries[index][None], key_blocks[None], value_blocks[None], attn_prob, prob_low, out_grad[index][None])
        key_acc = key_acc.at[clipped].add(key_grad[0].astype(jnp.float32) * valid_mask[:, None, None])
        value_acc = value_acc.at[clipped].add(value_grad[0].astype(jnp.float32) * valid_mask[:, None, None])
        return ((key_acc, value_acc), (mixed[0], query_grad[0]))
    zeros_acc = jnp.zeros((frames, tile_len, inner_width), jnp.float32)
    (key_acc, value_acc), (mixed, query_grad) = lax.scan(frame_step, (zeros_acc, zeros_acc), jnp.arange(frames, dtype=jnp.int32))
    layer_out = jnp.dot(mixed.reshape(-1, inner_width), w_out, preferred_element_type=jnp.float32)
    layer_out = layer_out.astype(jnp.bfloat16).reshape(frames, tile_len, width)
    key_sum = key_acc.astype(jnp.bfloat16).reshape(-1, inner_width)
    value_sum = value_acc.astype(jnp.bfloat16).reshape(-1, inner_width)
    total = jnp.dot(query_grad.reshape(-1, inner_width), w_query.T, preferred_element_type=jnp.float32)
    total = total + jnp.dot(key_sum, w_key.T, preferred_element_type=jnp.float32)
    total = total + jnp.dot(value_sum, w_value.T, preferred_element_type=jnp.float32)
    return (layer_out, total.astype(jnp.bfloat16).reshape(frames, tile_len, width))
```

```python
import functools
import math

import jax
import jax.numpy as jnp
from jax import lax
from jax.experimental import pallas as pl
from jax.experimental.pallas import tpu as pltpu
from jax.sharding import PartitionSpec as P

HEADS = 24
GROUP = 4
CHUNK = 8
NT = (((1,), (1,)), ((), ()))
NN = (((1,), (0,)), ((), ()))
TN = (((0,), (0,)), ((), ()))
MESH = pl.DeviceIdType.MESH


def dot(a, b, dims):
    return lax.dot_general(a, b, dims, preferred_element_type=jnp.float32)


def layer_kernel(
    count, frames, mem, tile, head_dim, steps,
    ids, recalled, tiles, x_ref, cot_hbm, wq_hbm, wo_hbm, wk_hbm, wv_hbm,
    layer_ref, grad_ref,
    weights, cot_ref, q_ref, g_ref, k_ext, v_ext, k_mem, v_mem, want_out, want_in, choose,
    rows_out, rows_in, mixed, query_grad, sums, blocks, gathered, outgoing, incoming, total,
    spots, place,
    weight_sem, cot_sem, want_send, want_recv, row_send, row_recv, halo_send, halo_recv,
    send_sem, recv_sem, edge_send, edge_recv,
):
    me = lax.axis_index("tm")
    width = x_ref.shape[1]
    own = x_ref.shape[0]
    cols = q_ref.shape[1] // steps
    wide = 2 * cols
    chunks = count // CHUNK
    entries = frames * mem
    scale = 1.0 / math.sqrt(head_dim)
    loads = [
        pltpu.make_async_copy(source, weights.at[i], weight_sem.at[i])
        for i, source in enumerate((wq_hbm, wo_hbm, wk_hbm, wv_hbm))
    ]
    load_cot = pltpu.make_async_copy(cot_hbm, cot_ref, cot_sem)
    loads[0].start()
    load_cot.start()
    for load in loads[1:]:
        load.start()

    def shift(i):
        half = i // 2
        return count // 2 + (i % 2) * 2 * half - half

    def peer(i):
        return {"tm": lax.rem(me + shift(i), count)}

    def asker(i):
        return {"tm": lax.rem(me + count - shift(i), count)}

    def beside(side):
        return {"tm": lax.rem(me + (1 if side == 0 else count - 1), count)}

    barrier = pltpu.get_barrier_semaphore()

    @pl.loop(1, count)
    def _(i):
        pl.semaphore_signal(barrier, inc=1, device_id=peer(i), device_id_type=MESH)

    slots = []
    slot_at = lax.broadcasted_iota(jnp.int32, want_out.shape, 0)
    asked = jnp.full(want_out.shape, -frames, jnp.int32)
    for e in range(entries):
        frame = ids[e // mem, e % mem]
        away = lax.rem(lax.div(frame, frames) - me + count, count)
        slot = jnp.where(
            away >= count // 2, 2 * away - count + 1, lax.rem(count - 2 * away, count)
        )
        spots[e] = slot
        slots.append(slot)
        asked = jnp.where(slot_at == slot, lax.rem(frame, frames), asked)
    want_out[...] = asked

    pl.semaphore_wait(barrier, count - 1)

    def ask(i):
        return pltpu.make_async_remote_copy(
            src_ref=want_out.at[i], dst_ref=want_in.at[i], send_sem=want_send,
            recv_sem=want_recv, device_id=peer(i), device_id_type=MESH,
        )

    def push_halo(side):
        return pltpu.make_async_remote_copy(
            src_ref=x_ref.at[pl.ds((frames - 1) * tile if side == 0 else 0, tile)],
            dst_ref=rows_in.at[count + side],
            send_sem=halo_send.at[side], recv_sem=halo_recv.at[side],
            device_id=beside(side), device_id_type=MESH,
        )

    def push_row(i, c):
        return pltpu.make_async_remote_copy(
            src_ref=rows_out.at[i], dst_ref=rows_in.at[i], send_sem=row_send,
            recv_sem=row_recv.at[c], device_id=asker(i), device_id_type=MESH,
        )

    @pl.loop(1, count)
    def _(i):
        ask(i).start()

    push_halo(0).start()
    push_halo(1).start()
    want_in[0] = want_out[0]
    others = pl.ds(1, count - 1)
    pltpu.make_async_copy(want_in.at[others], want_in.at[others], want_recv).wait()

    shape = (CHUNK, tile, own)
    token = lax.broadcasted_iota(jnp.int32, shape, 1)
    lane = lax.broadcasted_iota(jnp.int32, shape, 2)

    def pick_rows(c):
        asked = want_in[pl.ds(c * CHUNK, CHUNK)][:, 0:1, :]
        hot = jnp.where(lane == asked * tile + token, 1.0, 0.0).reshape(CHUNK * tile, own)
        low = hot.astype(jnp.bfloat16)
        for part in range(width // wide):
            lanes = slice(part * wide, (part + 1) * wide)
            rows_out[pl.ds(c * CHUNK, CHUNK), :, lanes] = (
                dot(low, x_ref[:, lanes], NN).astype(jnp.bfloat16).reshape(CHUNK, tile, wide)
            )
        return hot

    hots = []
    for c in range(chunks):
        hots.append(pick_rows(c))

        @pl.loop(1 if c == 0 else 0, CHUNK)
        def _(i):
            push_row(c * CHUNK + i, c).start()

    rows_in[0] = rows_out[0]
    for c in range(chunks):
        choose[:, c * CHUNK * tile : (c + 1) * CHUNK * tile] = hots[c].T.astype(jnp.bfloat16)
    edge_row = lax.broadcasted_iota(jnp.int32, (own, 2 * tile), 0)
    edge_lane = lax.broadcasted_iota(jnp.int32, (own, 2 * tile), 1)
    edge_spot = jnp.where(edge_lane < tile, edge_lane, edge_lane + (frames - 2) * tile)
    choose[:, count * tile : (count + 2) * tile] = jnp.where(
        edge_row == edge_spot, 1.0, 0.0
    ).astype(jnp.bfloat16)

    for i in range(count):
        at = jnp.int32(0)
        for e in range(entries):
            at = jnp.where(slots[e] == i, e, at)
        place[i] = at

    loads[0].wait()

    @pl.loop(0, width // wide)
    def _(p):
        lanes = pl.ds(pl.multiple_of(p * wide, wide), wide)
        q_ref[:, lanes] = dot(x_ref[...], weights[0, :, lanes], NN).astype(jnp.bfloat16)

    load_cot.wait()
    loads[1].wait()

    @pl.loop(0, width // wide)
    def _(p):
        lanes = pl.ds(pl.multiple_of(p * wide, wide), wide)
        g_ref[:, lanes] = dot(cot_ref[...], weights[1, lanes, :], NT).astype(jnp.bfloat16)

    push_halo(0).wait_recv()
    push_halo(1).wait_recv()
    loads[2].wait()
    loads[3].wait()

    @pl.loop(0, width // wide)
    def _(p):
        lanes = pl.ds(pl.multiple_of(p * wide, wide), wide)
        ext = jnp.concatenate([rows_in[count], x_ref[...], rows_in[count + 1]], axis=0)
        k_ext[:, lanes] = dot(ext, weights[2, :, lanes], NN).astype(jnp.bfloat16)
        v_ext[:, lanes] = dot(ext, weights[3, :, lanes], NN).astype(jnp.bfloat16)

    def project(c):
        some = pl.ds(c * CHUNK, CHUNK)

        @pl.loop(0, width // wide)
        def _(p):
            lanes = pl.ds(pl.multiple_of(p * wide, wide), wide)
            flat = rows_in[some].reshape(CHUNK * tile, width)
            for weight, far in ((2, k_mem), (3, v_mem)):
                far[some, :, lanes] = (
                    dot(flat, weights[weight, :, lanes], NN)
                    .astype(jnp.bfloat16)
                    .reshape(CHUNK, tile, wide)
                )

    first = pl.ds(1, CHUNK - 1)
    pltpu.make_async_copy(rows_in.at[first], rows_in.at[first], row_recv.at[0]).wait()
    project(0)

    @pl.loop(1, chunks)
    def _(c):
        some = pl.ds(c * CHUNK, CHUNK)
        pltpu.make_async_copy(rows_in.at[some], rows_in.at[some], row_recv.at[c]).wait()
        project(c)

    rows = GROUP * tile
    own_head = (
        lax.broadcasted_iota(jnp.int32, (rows, cols), 0) // tile
        == lax.broadcasted_iota(jnp.int32, (rows, cols), 1) // head_dim
    )
    head_at = lax.broadcasted_iota(jnp.int32, (tile, cols), 1) // head_dim

    def spread(block):
        tall = jnp.concatenate([block] * GROUP, axis=0)
        return jnp.where(own_head, tall, jnp.zeros_like(tall))

    def fold(tall):
        flat = tall[0:tile]
        for part in range(1, GROUP):
            flat = jnp.where(head_at == part, tall[part * tile : (part + 1) * tile], flat)
        return flat

    def hide(f):
        frame = me * frames + f
        lower = (frame >= 1) & (tiles[0, f] == 1)
        upper = (frame < frames * count - 1) & (tiles[1, f] == 1)
        kept = [lower, None, upper] + [recalled[f] > j for j in range(mem)]
        return [None if k is None else jnp.where(k, 0.0, -1e30) for k in kept]

    def attend(g):
        lanes = pl.ds(pl.multiple_of(g * cols, cols), cols)
        held = [None, None]
        late = [None, None]
        for f in range(frames):
            here = slice(f * tile, (f + 1) * tile)
            near = slice(f * tile, (f + 3) * tile)

            def gather(ext, far):
                return jnp.concatenate(
                    [ext[near, lanes]] + [far[spots[f * mem + j], :, lanes] for j in range(mem)],
                    axis=0,
                )

            keys = gather(k_ext, k_mem)
            values = gather(v_ext, v_mem)
            queries = spread(q_ref[here, lanes] * scale)
            grads = spread(g_ref[here, lanes])
            scores = dot(keys, queries, NT)
            scores = jnp.concatenate(
                [
                    part if bias is None else part + bias
                    for bias, part in zip(hide(f), jnp.split(scores, 3 + mem, axis=0))
                ],
                axis=0,
            )
            expo = jnp.exp(scores - jnp.max(scores, axis=0, keepdims=True))
            prob = expo * (1.0 / jnp.sum(expo, axis=0, keepdims=True))
            low = prob.astype(jnp.bfloat16)
            prob_grad = dot(values, grads, NT)
            delta = jnp.sum(prob * prob_grad, axis=0, keepdims=True)
            score_grad = (prob * (prob_grad - delta)).astype(jnp.bfloat16)
            mixed[here, lanes] = fold(dot(low, values, TN)).astype(jnp.bfloat16)
            query_grad[here, lanes] = (fold(dot(score_grad, keys, TN)) * scale).astype(
                jnp.bfloat16
            )
            parts = (
                dot(score_grad, queries, NN).astype(jnp.bfloat16),
                dot(low, grads, NN).astype(jnp.bfloat16),
            )
            for kv, part in enumerate(parts):
                before = part[0:tile]
                middle = part[tile : 2 * tile].astype(jnp.float32)
                after = part[2 * tile : 3 * tile]
                if f == 0:
                    blocks[entries + 1, kv, :, lanes] = before
                else:
                    back = slice((f - 1) * tile, f * tile)
                    sums[kv, back, lanes] = (held[kv] + before.astype(jnp.float32)).astype(
                        jnp.bfloat16
                    )
                    middle = middle + late[kv]
                if f == frames - 1:
                    blocks[entries, kv, :, lanes] = after
                    sums[kv, here, lanes] = middle.astype(jnp.bfloat16)
                held[kv] = middle
                late[kv] = after.astype(jnp.float32)
                for j in range(mem):
                    blocks[f * mem + j, kv, :, lanes] = part[(3 + j) * tile : (4 + j) * tile]

    @pl.loop(0, steps)
    def _(g):
        attend(g)

    def push(i, c):
        return pltpu.make_async_remote_copy(
            src_ref=outgoing.at[i], dst_ref=incoming.at[i], send_sem=send_sem,
            recv_sem=recv_sem.at[c], device_id=peer(i), device_id_type=MESH,
        )

    def push_edge(side):
        return pltpu.make_async_remote_copy(
            src_ref=outgoing.at[count + side], dst_ref=incoming.at[count + side],
            send_sem=edge_send.at[side], recv_sem=edge_recv.at[side],
            device_id=beside(side), device_id_type=MESH,
        )

    for c in range(chunks):
        start = c * CHUNK
        size = CHUNK if c < chunks - 1 else CHUNK + 2
        for n in range(size):
            source = place[start + n] if n < CHUNK else entries + n - CHUNK
            for kv in range(2):
                gathered[kv, n * tile : (n + 1) * tile, :] = blocks[source, kv]
        for part in range(width // wide):
            lanes = slice(part * wide, (part + 1) * wide)
            total_rows = dot(gathered[0, : size * tile], weights[2, lanes, :], NT)
            total_rows += dot(gathered[1, : size * tile], weights[3, lanes, :], NT)
            outgoing[start : start + size, :, lanes] = total_rows.astype(jnp.bfloat16).reshape(
                size, tile, wide
            )

        @pl.loop(1 if c == 0 else 0, CHUNK)
        def _(i):
            push(start + i, c).start()

    push_edge(0).start()
    push_edge(1).start()
    incoming[0] = outgoing[0]

    for part in range(width // wide):
        lanes = slice(part * wide, (part + 1) * wide)
        layer_ref[:, lanes] = dot(mixed[...], weights[1, :, lanes], NN).astype(jnp.bfloat16)
        total[:, lanes] = (
            dot(query_grad[...], weights[0, lanes, :], NT)
            + dot(sums[0], weights[2, lanes, :], NT)
            + dot(sums[1], weights[3, lanes, :], NT)
        )

    for c in range(chunks):
        some = pl.ds(1, CHUNK - 1) if c == 0 else pl.ds(c * CHUNK, CHUNK)
        pltpu.make_async_copy(incoming.at[some], incoming.at[some], recv_sem.at[c]).wait()
        start = c * CHUNK
        size = CHUNK
        if c == chunks - 1:
            push_edge(0).wait_recv()
            push_edge(1).wait_recv()
            size += 2
        for part in range(width // wide):
            lanes = slice(part * wide, (part + 1) * wide)
            came = incoming[start : start + size, :, lanes].reshape(size * tile, wide)
            whole = total[:, lanes] + dot(
                choose[:, start * tile : (start + size) * tile], came, NN
            )
            if c == chunks - 1:
                grad_ref[:, lanes] = whole.astype(jnp.bfloat16)
            else:
                total[:, lanes] = whole

    pltpu.make_async_copy(want_out.at[others], want_out.at[others], want_send).wait()
    pltpu.make_async_copy(rows_out.at[others], rows_out.at[others], row_send).wait()
    pltpu.make_async_copy(outgoing.at[others], outgoing.at[others], send_sem).wait()
    push_halo(0).wait_send()
    push_halo(1).wait_send()
    push_edge(0).wait_send()
    push_edge(1).wait_send()


def on_device(
    latents, w_query, w_key, w_value, w_out, cotangent, memory_ids, memory_count, tile_mask
):
    frames, tile, width = latents.shape
    count = lax.axis_size("tm")
    rows = latents.reshape(-1, width)
    mem = memory_ids.shape[1]
    inner = w_query.shape[1]
    head_dim = inner // HEADS
    cols = GROUP * head_dim
    steps = inner // cols
    own = frames * tile
    chunks = count // CHUNK

    vmem = pl.BlockSpec(memory_space=pltpu.VMEM)
    smem = pl.BlockSpec(memory_space=pltpu.SMEM)
    hbm = pl.BlockSpec(memory_space=pl.ANY)
    layer_out, latent_grad = pl.pallas_call(
        functools.partial(layer_kernel, count, frames, mem, tile, head_dim, steps),
        in_specs=[smem] * 3 + [vmem] + [hbm] * 5,
        out_specs=[vmem, vmem],
        out_shape=[
            jax.ShapeDtypeStruct((own, width), jnp.bfloat16),
            jax.ShapeDtypeStruct((own, width), jnp.bfloat16),
        ],
        scratch_shapes=[
            pltpu.VMEM((4, width, inner), jnp.bfloat16),
            pltpu.VMEM((own, width), jnp.bfloat16),
            pltpu.VMEM((own, inner), jnp.bfloat16),
            pltpu.VMEM((own, inner), jnp.bfloat16),
            pltpu.VMEM((own + 2 * tile, inner), jnp.bfloat16),
            pltpu.VMEM((own + 2 * tile, inner), jnp.bfloat16),
            pltpu.VMEM((count, tile, inner), jnp.bfloat16),
            pltpu.VMEM((count, tile, inner), jnp.bfloat16),
            pltpu.VMEM((count, 8, own), jnp.int32),
            pltpu.VMEM((count, 8, own), jnp.int32),
            pltpu.VMEM((own, (count + 2) * tile), jnp.bfloat16),
            pltpu.VMEM((count, tile, width), jnp.bfloat16),
            pltpu.VMEM((count + 2, tile, width), jnp.bfloat16),
            pltpu.VMEM((own, inner), jnp.bfloat16),
            pltpu.VMEM((own, inner), jnp.bfloat16),
            pltpu.VMEM((2, own, inner), jnp.bfloat16),
            pltpu.VMEM((frames * mem + 2, 2, tile, inner), jnp.bfloat16),
            pltpu.VMEM((2, (CHUNK + 2) * tile, inner), jnp.bfloat16),
            pltpu.VMEM((count + 2, tile, width), jnp.bfloat16),
            pltpu.VMEM((count + 2, tile, width), jnp.bfloat16),
            pltpu.VMEM((own, width), jnp.float32),
            pltpu.SMEM((frames * mem,), jnp.int32),
            pltpu.SMEM((count,), jnp.int32),
            pltpu.SemaphoreType.DMA((4,)),
            pltpu.SemaphoreType.DMA,
            pltpu.SemaphoreType.DMA,
            pltpu.SemaphoreType.DMA,
            pltpu.SemaphoreType.DMA,
            pltpu.SemaphoreType.DMA((chunks,)),
            pltpu.SemaphoreType.DMA((2,)),
            pltpu.SemaphoreType.DMA((2,)),
            pltpu.SemaphoreType.DMA,
            pltpu.SemaphoreType.DMA((chunks,)),
            pltpu.SemaphoreType.DMA((2,)),
            pltpu.SemaphoreType.DMA((2,)),
        ],
        compiler_params=pltpu.CompilerParams(
            collective_id=0, has_side_effects=True, vmem_limit_bytes=58 * 2**20
        ),
    )(
        memory_ids, memory_count, tile_mask.T, rows, cotangent.reshape(-1, width),
        w_query, w_out, w_key, w_value,
    )
    return (
        layer_out.reshape(frames, tile, width),
        latent_grad.reshape(frames, tile, width),
    )


def solution(mesh):
    placed = (
        P(("shard", "tm"), None, None),
        P(),
        P(),
        P(),
        P(),
        P(("shard", "tm"), None, None),
        P(("shard", "tm"), None),
        P(("shard", "tm")),
        P(("shard", "tm"), None),
    )
    return jax.shard_map(
        on_device,
        mesh=mesh,
        in_specs=placed,
        out_specs=(P(("shard", "tm"), None, None), P(("shard", "tm"), None, None)),
        check_vma=False,
    )
```

```python
import functools
import math

import jax
import jax.numpy as jnp
from jax import lax
from jax.experimental import pallas as pl
from jax.experimental.pallas import tpu as pltpu
from jax.sharding import PartitionSpec as P

HEADS = 24
GROUP = 4
CHUNK = 8
NT = (((1,), (1,)), ((), ()))
NN = (((1,), (0,)), ((), ()))
TN = (((0,), (0,)), ((), ()))
MESH = pl.DeviceIdType.MESH


def dot(a, b, dims):
    return lax.dot_general(a, b, dims, preferred_element_type=jnp.float32)


def layer_kernel(
    count, frames, mem, tile, head_dim, steps,
    ids, recalled, tiles, x_ref, cot_hbm, wq_hbm, wo_hbm, wk_hbm, wv_hbm,
    layer_ref, grad_ref,
    weights, cot_ref, q_ref, g_ref, k_ext, v_ext, k_mem, v_mem, want_out, want_in, choose,
    rows_out, rows_in, x_far, mixed, query_grad, sums, blocks, gathered, outgoing, incoming,
    relay_out, relay_in, total,
    spots, place,
    weight_sem, cot_sem, want_send, want_recv, row_send, row_recv, halo_send, halo_recv,
    send_sem, recv_sem, edge_send, edge_recv, far_send, far_recv, relay_send, relay_recv,
):
    me = lax.axis_index("tm")
    width = x_ref.shape[1]
    own = x_ref.shape[0]
    cols = q_ref.shape[1] // steps
    wide = 2 * cols
    half = count // 2
    chunks = count // CHUNK
    near_chunks = half // CHUNK
    place_in = lax.rem(me, half)
    base = me - place_in
    entries = frames * mem
    scale = 1.0 / math.sqrt(head_dim)
    loads = [
        pltpu.make_async_copy(source, weights.at[i], weight_sem.at[i])
        for i, source in enumerate((wq_hbm, wo_hbm, wk_hbm, wv_hbm))
    ]
    load_cot = pltpu.make_async_copy(cot_hbm, cot_ref, cot_sem)
    loads[0].start()
    load_cot.start()
    for load in loads[1:]:
        load.start()

    def mate(i):
        return {"tm": base + lax.rem(place_in + i, half)}

    def asker(i):
        return {"tm": base + lax.rem(place_in + half - i, half)}

    partner = {"tm": lax.rem(me + half, count)}

    def beside(side):
        return {"tm": lax.rem(me + (1 if side == 0 else count - 1), count)}

    barrier = pltpu.get_barrier_semaphore()

    @pl.loop(1, count)
    def _(i):
        pl.semaphore_signal(
            barrier, inc=1, device_id={"tm": lax.rem(me + i, count)}, device_id_type=MESH
        )

    slots = []
    slot_at = lax.broadcasted_iota(jnp.int32, want_out.shape, 0)
    slot_at += half * lax.broadcasted_iota(jnp.int32, want_out.shape, 1)
    asked = jnp.full(want_out.shape, -frames, jnp.int32)
    for e in range(entries):
        frame = ids[e // mem, e % mem]
        owner = lax.div(frame, frames)
        away = lax.rem(owner - place_in + count, half)
        same = (owner >= base) & (owner < base + half)
        slot = away + jnp.where(same, 0, half)
        spots[e] = slot
        slots.append(slot)
        asked = jnp.where(slot_at == slot, lax.rem(frame, frames), asked)
    want_out[...] = asked

    pl.semaphore_wait(barrier, count - 1)

    def ask(i):
        return pltpu.make_async_remote_copy(
            src_ref=want_out.at[i], dst_ref=want_in.at[i], send_sem=want_send,
            recv_sem=want_recv, device_id=mate(i), device_id_type=MESH,
        )

    def push_halo(side):
        return pltpu.make_async_remote_copy(
            src_ref=x_ref.at[pl.ds((frames - 1) * tile if side == 0 else 0, tile)],
            dst_ref=rows_in.at[count + side],
            send_sem=halo_send.at[side], recv_sem=halo_recv.at[side],
            device_id=beside(side), device_id_type=MESH,
        )

    swap = pltpu.make_async_remote_copy(
        src_ref=x_ref, dst_ref=x_far, send_sem=far_send, recv_sem=far_recv,
        device_id=partner, device_id_type=MESH,
    )

    def push_row(i, c):
        return pltpu.make_async_remote_copy(
            src_ref=rows_out.at[i], dst_ref=rows_in.at[i], send_sem=row_send,
            recv_sem=row_recv.at[c], device_id=asker(lax.rem(i, half)), device_id_type=MESH,
        )

    def remote_slots(c):
        start = c * CHUNK
        return start + (1 if start % half == 0 else 0), start + CHUNK

    @pl.loop(1, half)
    def _(i):
        ask(i).start()

    swap.start()
    push_halo(0).start()
    push_halo(1).start()
    want_in[0] = want_out[0]
    mates = pl.ds(1, half - 1)
    pltpu.make_async_copy(want_in.at[mates], want_in.at[mates], want_recv).wait()

    shape = (CHUNK, tile, own)
    token = lax.broadcasted_iota(jnp.int32, shape, 1)
    lane = lax.broadcasted_iota(jnp.int32, shape, 2)

    def pick_rows(c):
        some = pl.ds(c * CHUNK, CHUNK)
        far = c // near_chunks
        asked = want_in[c % near_chunks * CHUNK : (c % near_chunks + 1) * CHUNK, far, 0:1, :]
        hot = jnp.where(lane == asked * tile + token, 1.0, 0.0).reshape(CHUNK * tile, own)
        low = hot.astype(jnp.bfloat16)
        source = x_far if far else x_ref
        for part in range(width // wide):
            lanes = slice(part * wide, (part + 1) * wide)
            rows_out[some, :, lanes] = (
                dot(low, source[:, lanes], NN).astype(jnp.bfloat16).reshape(CHUNK, tile, wide)
            )
        start, stop = remote_slots(c)

        @pl.loop(start, stop)
        def _(i):
            push_row(i, c).start()

        if start != c * CHUNK:
            rows_in[c * CHUNK] = rows_out[c * CHUNK]
        choose[:, c * CHUNK * tile : (c + 1) * CHUNK * tile] = hot.T.astype(jnp.bfloat16)

    for c in range(near_chunks):
        pick_rows(c)

    edge_row = lax.broadcasted_iota(jnp.int32, (own, 2 * tile), 0)
    edge_lane = lax.broadcasted_iota(jnp.int32, (own, 2 * tile), 1)
    edge_spot = jnp.where(edge_lane < tile, edge_lane, edge_lane + (frames - 2) * tile)
    choose[:, count * tile : (count + 2) * tile] = jnp.where(
        edge_row == edge_spot, 1.0, 0.0
    ).astype(jnp.bfloat16)

    for i in range(count):
        at = jnp.int32(0)
        for e in range(entries):
            at = jnp.where(slots[e] == i, e, at)
        place[i] = at

    loads[0].wait()

    @pl.loop(0, width // wide)
    def _(p):
        lanes = pl.ds(pl.multiple_of(p * wide, wide), wide)
        q_ref[:, lanes] = dot(x_ref[...], weights[0, :, lanes], NN).astype(jnp.bfloat16)

    load_cot.wait()
    loads[1].wait()

    @pl.loop(0, width // wide)
    def _(p):
        lanes = pl.ds(pl.multiple_of(p * wide, wide), wide)
        g_ref[:, lanes] = dot(cot_ref[...], weights[1, lanes, :], NT).astype(jnp.bfloat16)

    push_halo(0).wait_recv()
    push_halo(1).wait_recv()
    loads[2].wait()
    loads[3].wait()

    @pl.loop(0, width // wide)
    def _(p):
        lanes = pl.ds(pl.multiple_of(p * wide, wide), wide)
        ext = jnp.concatenate([rows_in[count], x_ref[...], rows_in[count + 1]], axis=0)
        k_ext[:, lanes] = dot(ext, weights[2, :, lanes], NN).astype(jnp.bfloat16)
        v_ext[:, lanes] = dot(ext, weights[3, :, lanes], NN).astype(jnp.bfloat16)

    def project(c):
        start, stop = remote_slots(c)
        came = pl.ds(start, stop - start)
        pltpu.make_async_copy(rows_in.at[came], rows_in.at[came], row_recv.at[c]).wait()
        some = pl.ds(c * CHUNK, CHUNK)

        @pl.loop(0, width // wide)
        def _(p):
            lanes = pl.ds(pl.multiple_of(p * wide, wide), wide)
            flat = rows_in[some].reshape(CHUNK * tile, width)
            for weight, far in ((2, k_mem), (3, v_mem)):
                far[some, :, lanes] = (
                    dot(flat, weights[weight, :, lanes], NN)
                    .astype(jnp.bfloat16)
                    .reshape(CHUNK, tile, wide)
                )

    swap.wait_recv()
    for c in range(near_chunks, chunks):
        pick_rows(c)
    for c in range(chunks):
        project(c)

    rows = GROUP * tile
    own_head = (
        lax.broadcasted_iota(jnp.int32, (rows, cols), 0) // tile
        == lax.broadcasted_iota(jnp.int32, (rows, cols), 1) // head_dim
    )
    head_at = lax.broadcasted_iota(jnp.int32, (tile, cols), 1) // head_dim

    def spread(block):
        tall = jnp.concatenate([block] * GROUP, axis=0)
        return jnp.where(own_head, tall, jnp.zeros_like(tall))

    def fold(tall):
        flat = tall[0:tile]
        for part in range(1, GROUP):
            flat = jnp.where(head_at == part, tall[part * tile : (part + 1) * tile], flat)
        return flat

    def hide(f):
        frame = me * frames + f
        lower = (frame >= 1) & (tiles[0, f] == 1)
        upper = (frame < frames * count - 1) & (tiles[1, f] == 1)
        kept = [lower, None, upper] + [recalled[f] > j for j in range(mem)]
        return [None if k is None else jnp.where(k, 0.0, -1e30) for k in kept]

    def attend(g):
        lanes = pl.ds(pl.multiple_of(g * cols, cols), cols)
        held = [None, None]
        late = [None, None]
        for f in range(frames):
            here = slice(f * tile, (f + 1) * tile)
            near = slice(f * tile, (f + 3) * tile)

            def gather(ext, far):
                return jnp.concatenate(
                    [ext[near, lanes]] + [far[spots[f * mem + j], :, lanes] for j in range(mem)],
                    axis=0,
                )

            keys = gather(k_ext, k_mem)
            values = gather(v_ext, v_mem)
            queries = spread(q_ref[here, lanes] * scale)
            grads = spread(g_ref[here, lanes])
            scores = dot(keys, queries, NT)
            scores = jnp.concatenate(
                [
                    part if bias is None else part + bias
                    for bias, part in zip(hide(f), jnp.split(scores, 3 + mem, axis=0))
                ],
                axis=0,
            )
            expo = jnp.exp(scores - jnp.max(scores, axis=0, keepdims=True))
            prob = expo * (1.0 / jnp.sum(expo, axis=0, keepdims=True))
            low = prob.astype(jnp.bfloat16)
            prob_grad = dot(values, grads, NT)
            delta = jnp.sum(prob * prob_grad, axis=0, keepdims=True)
            score_grad = (prob * (prob_grad - delta)).astype(jnp.bfloat16)
            mixed[here, lanes] = fold(dot(low, values, TN)).astype(jnp.bfloat16)
            query_grad[here, lanes] = (fold(dot(score_grad, keys, TN)) * scale).astype(
                jnp.bfloat16
            )
            parts = (
                dot(score_grad, queries, NN).astype(jnp.bfloat16),
                dot(low, grads, NN).astype(jnp.bfloat16),
            )
            for kv, part in enumerate(parts):
                before = part[0:tile]
                middle = part[tile : 2 * tile].astype(jnp.float32)
                after = part[2 * tile : 3 * tile]
                if f == 0:
                    blocks[entries + 1, kv, :, lanes] = before
                else:
                    back = slice((f - 1) * tile, f * tile)
                    sums[kv, back, lanes] = (held[kv] + before.astype(jnp.float32)).astype(
                        jnp.bfloat16
                    )
                    middle = middle + late[kv]
                if f == frames - 1:
                    blocks[entries, kv, :, lanes] = after
                    sums[kv, here, lanes] = middle.astype(jnp.bfloat16)
                held[kv] = middle
                late[kv] = after.astype(jnp.float32)
                for j in range(mem):
                    blocks[f * mem + j, kv, :, lanes] = part[(3 + j) * tile : (4 + j) * tile]

    @pl.loop(0, steps)
    def _(g):
        attend(g)

    def push(i, c):
        return pltpu.make_async_remote_copy(
            src_ref=outgoing.at[i], dst_ref=incoming.at[i], send_sem=send_sem,
            recv_sem=recv_sem.at[c], device_id=mate(lax.rem(i, half)), device_id_type=MESH,
        )

    relay = pltpu.make_async_remote_copy(
        src_ref=relay_out, dst_ref=relay_in, send_sem=relay_send, recv_sem=relay_recv,
        device_id=partner, device_id_type=MESH,
    )

    def push_edge(side):
        return pltpu.make_async_remote_copy(
            src_ref=outgoing.at[count + side], dst_ref=incoming.at[count + side],
            send_sem=edge_send.at[side], recv_sem=edge_recv.at[side],
            device_id=beside(side), device_id_type=MESH,
        )

    for c in list(range(near_chunks, chunks)) + list(range(near_chunks)):
        start = c * CHUNK
        extra = 2 if c == near_chunks - 1 else 0
        for n in range(CHUNK + extra):
            source = place[start + n] if n < CHUNK else entries + n - CHUNK
            for kv in range(2):
                gathered[kv, n * tile : (n + 1) * tile, :] = blocks[source, kv]
        taken = (CHUNK + extra) * tile
        for part in range(width // wide):
            lanes = slice(part * wide, (part + 1) * wide)
            sent = dot(gathered[0, :taken], weights[2, lanes, :], NT)
            sent += dot(gathered[1, :taken], weights[3, lanes, :], NT)
            sent = sent.astype(jnp.bfloat16).reshape(CHUNK + extra, tile, wide)
            outgoing[start : start + CHUNK, :, lanes] = sent[:CHUNK]
            if extra:
                outgoing[count : count + 2, :, lanes] = sent[CHUNK:]
        first, stop = remote_slots(c)

        @pl.loop(first, stop)
        def _(i):
            push(i, c).start()

        if first != start:
            incoming[start] = outgoing[start]

    push_edge(0).start()
    push_edge(1).start()

    def await_chunk(c):
        start, stop = remote_slots(c)
        came = pl.ds(start, stop - start)
        pltpu.make_async_copy(incoming.at[came], incoming.at[came], recv_sem.at[c]).wait()

    for c in range(near_chunks, chunks):
        await_chunk(c)
    for part in range(width // wide):
        lanes = slice(part * wide, (part + 1) * wide)
        came = incoming[half:count, :, lanes].reshape(half * tile, wide)
        relay_out[:, lanes] = dot(choose[:, half * tile : count * tile], came, NN).astype(
            jnp.bfloat16
        )
    relay.start()

    for part in range(width // wide):
        lanes = slice(part * wide, (part + 1) * wide)
        layer_ref[:, lanes] = dot(mixed[...], weights[1, :, lanes], NN).astype(jnp.bfloat16)
        total[:, lanes] = (
            dot(query_grad[...], weights[0, lanes, :], NT)
            + dot(sums[0], weights[2, lanes, :], NT)
            + dot(sums[1], weights[3, lanes, :], NT)
        )

    for c in range(near_chunks):
        await_chunk(c)
    push_edge(0).wait_recv()
    push_edge(1).wait_recv()
    for part in range(width // wide):
        lanes = slice(part * wide, (part + 1) * wide)
        came = incoming[0:half, :, lanes].reshape(half * tile, wide)
        edges = incoming[count : count + 2, :, lanes].reshape(2 * tile, wide)
        total[:, lanes] += dot(choose[:, : half * tile], came, NN) + dot(
            choose[:, count * tile :], edges, NN
        )
    relay.wait_recv()
    grad_ref[...] = (total[...] + relay_in[...].astype(jnp.float32)).astype(jnp.bfloat16)

    pltpu.make_async_copy(want_out.at[mates], want_out.at[mates], want_send).wait()
    sent_rows = pl.ds(0, count - 2)
    pltpu.make_async_copy(rows_out.at[sent_rows], rows_out.at[sent_rows], row_send).wait()
    pltpu.make_async_copy(outgoing.at[sent_rows], outgoing.at[sent_rows], send_sem).wait()
    swap.wait_send()
    relay.wait_send()
    push_halo(0).wait_send()
    push_halo(1).wait_send()
    push_edge(0).wait_send()
    push_edge(1).wait_send()


def on_device(
    latents, w_query, w_key, w_value, w_out, cotangent, memory_ids, memory_count, tile_mask
):
    frames, tile, width = latents.shape
    count = lax.axis_size("tm")
    rows = latents.reshape(-1, width)
    mem = memory_ids.shape[1]
    inner = w_query.shape[1]
    head_dim = inner // HEADS
    cols = GROUP * head_dim
    steps = inner // cols
    own = frames * tile
    chunks = count // CHUNK

    vmem = pl.BlockSpec(memory_space=pltpu.VMEM)
    smem = pl.BlockSpec(memory_space=pltpu.SMEM)
    hbm = pl.BlockSpec(memory_space=pl.ANY)
    layer_out, latent_grad = pl.pallas_call(
        functools.partial(layer_kernel, count, frames, mem, tile, head_dim, steps),
        in_specs=[smem] * 3 + [vmem] + [hbm] * 5,
        out_specs=[vmem, vmem],
        out_shape=[
            jax.ShapeDtypeStruct((own, width), jnp.bfloat16),
            jax.ShapeDtypeStruct((own, width), jnp.bfloat16),
        ],
        scratch_shapes=[
            pltpu.VMEM((4, width, inner), jnp.bfloat16),
            pltpu.VMEM((own, width), jnp.bfloat16),
            pltpu.VMEM((own, inner), jnp.bfloat16),
            pltpu.VMEM((own, inner), jnp.bfloat16),
            pltpu.VMEM((own + 2 * tile, inner), jnp.bfloat16),
            pltpu.VMEM((own + 2 * tile, inner), jnp.bfloat16),
            pltpu.VMEM((count, tile, inner), jnp.bfloat16),
            pltpu.VMEM((count, tile, inner), jnp.bfloat16),
            pltpu.VMEM((count // 2, 2, 8, own), jnp.int32),
            pltpu.VMEM((count // 2, 2, 8, own), jnp.int32),
            pltpu.VMEM((own, (count + 2) * tile), jnp.bfloat16),
            pltpu.VMEM((count, tile, width), jnp.bfloat16),
            pltpu.VMEM((count + 2, tile, width), jnp.bfloat16),
            pltpu.VMEM((own, width), jnp.bfloat16),
            pltpu.VMEM((own, inner), jnp.bfloat16),
            pltpu.VMEM((own, inner), jnp.bfloat16),
            pltpu.VMEM((2, own, inner), jnp.bfloat16),
            pltpu.VMEM((frames * mem + 2, 2, tile, inner), jnp.bfloat16),
            pltpu.VMEM((2, (CHUNK + 2) * tile, inner), jnp.bfloat16),
            pltpu.VMEM((count + 2, tile, width), jnp.bfloat16),
            pltpu.VMEM((count + 2, tile, width), jnp.bfloat16),
            pltpu.VMEM((own, width), jnp.bfloat16),
            pltpu.VMEM((own, width), jnp.bfloat16),
            pltpu.VMEM((own, width), jnp.float32),
            pltpu.SMEM((frames * mem,), jnp.int32),
            pltpu.SMEM((count,), jnp.int32),
            pltpu.SemaphoreType.DMA((4,)),
            pltpu.SemaphoreType.DMA,
            pltpu.SemaphoreType.DMA,
            pltpu.SemaphoreType.DMA,
            pltpu.SemaphoreType.DMA,
            pltpu.SemaphoreType.DMA((chunks,)),
            pltpu.SemaphoreType.DMA((2,)),
            pltpu.SemaphoreType.DMA((2,)),
            pltpu.SemaphoreType.DMA,
            pltpu.SemaphoreType.DMA((chunks,)),
            pltpu.SemaphoreType.DMA((2,)),
            pltpu.SemaphoreType.DMA((2,)),
            pltpu.SemaphoreType.DMA,
            pltpu.SemaphoreType.DMA,
            pltpu.SemaphoreType.DMA,
            pltpu.SemaphoreType.DMA,
        ],
        compiler_params=pltpu.CompilerParams(
            collective_id=0, has_side_effects=True, vmem_limit_bytes=58 * 2**20
        ),
    )(
        memory_ids, memory_count, tile_mask.T, rows, cotangent.reshape(-1, width),
        w_query, w_out, w_key, w_value,
    )
    return (
        layer_out.reshape(frames, tile, width),
        latent_grad.reshape(frames, tile, width),
    )


def solution(mesh):
    placed = (
        P(("shard", "tm"), None, None),
        P(),
        P(),
        P(),
        P(),
        P(("shard", "tm"), None, None),
        P(("shard", "tm"), None),
        P(("shard", "tm")),
        P(("shard", "tm"), None),
    )
    return jax.shard_map(
        on_device,
        mesh=mesh,
        in_specs=placed,
        out_specs=(P(("shard", "tm"), None, None), P(("shard", "tm"), None, None)),
        check_vma=False,
    )
```

```python
import functools
import math

import jax
import jax.numpy as jnp
from jax import lax
from jax.experimental import pallas as pl
from jax.experimental.pallas import tpu as pltpu
from jax.sharding import PartitionSpec as P

HEADS = 24
GROUP = 4
NT = (((1,), (1,)), ((), ()))
NN = (((1,), (0,)), ((), ()))
TN = (((0,), (0,)), ((), ()))
MESH = pl.DeviceIdType.MESH


def dot(a, b, dims):
    return lax.dot_general(a, b, dims, preferred_element_type=jnp.float32)


def layer_kernel(
    count, frames, mem, tile, head_dim, steps,
    ids, recalled, tiles, x_ref, cot_hbm, wq_hbm, wo_hbm, wk_hbm, wv_hbm,
    layer_ref, grad_ref,
    weights, cot_ref, q_ref, g_ref, k_ext, v_ext, k_mem, v_mem, want_out, want_in, choose,
    rows_out, rows_in, far_out, far_in, x_far, far_sum, kept, mixed, query_grad, sums, blocks,
    gathered, near_in, back_in, relay_out, relay_in, total,
    spots, place,
    weight_sem, cot_sem, want_send, want_recv, row_send, row_recv, far_send, far_recv,
    halo_send, halo_recv, near_send, near_recv, back_send, back_recv, edge_send, edge_recv,
    swap_send, swap_recv, relay_send, relay_recv,
):
    me = lax.axis_index("tm")
    width = x_ref.shape[1]
    own = x_ref.shape[0]
    cols = q_ref.shape[1] // steps
    wide = 2 * cols
    half = count // 2
    pieces = width // wide
    cuts = [slice(p * wide, (p + 1) * wide) for p in range(pieces)]
    place_in = lax.rem(me, half)
    base = me - place_in
    entries = frames * mem
    scale = 1.0 / math.sqrt(head_dim)
    loads = [
        pltpu.make_async_copy(source, weights.at[i], weight_sem.at[i])
        for i, source in enumerate((wq_hbm, wo_hbm, wk_hbm, wv_hbm))
    ]
    load_cot = pltpu.make_async_copy(cot_hbm, cot_ref, cot_sem)
    loads[0].start()
    load_cot.start()
    for load in loads[1:]:
        load.start()

    def mate(i):
        return {"tm": base + lax.rem(place_in + i, half)}

    def asker(i):
        return {"tm": base + lax.rem(place_in + half - i, half)}

    partner = {"tm": lax.rem(me + half, count)}

    def beside(side):
        return {"tm": lax.rem(me + (1 if side == 0 else count - 1), count)}

    barrier = pltpu.get_barrier_semaphore()

    @pl.loop(1, count)
    def _(i):
        pl.semaphore_signal(
            barrier, inc=1, device_id={"tm": lax.rem(me + i, count)}, device_id_type=MESH
        )

    slots = []
    slot_at = lax.broadcasted_iota(jnp.int32, want_out.shape, 0)
    slot_at += half * lax.broadcasted_iota(jnp.int32, want_out.shape, 1)
    asked = jnp.full(want_out.shape, -frames, jnp.int32)
    for e in range(entries):
        frame = ids[e // mem, e % mem]
        owner = lax.div(frame, frames)
        away = lax.rem(owner - place_in + count, half)
        same = (owner >= base) & (owner < base + half)
        slot = away + jnp.where(same, 0, half)
        spots[e] = slot
        slots.append(slot)
        asked = jnp.where(slot_at == slot, lax.rem(frame, frames), asked)
    want_out[...] = asked

    pl.semaphore_wait(barrier, count - 1)

    def ask(i):
        return pltpu.make_async_remote_copy(
            src_ref=want_out.at[i], dst_ref=want_in.at[i], send_sem=want_send,
            recv_sem=want_recv, device_id=mate(i), device_id_type=MESH,
        )

    def push_halo(side):
        return pltpu.make_async_remote_copy(
            src_ref=x_ref.at[pl.ds((frames - 1) * tile if side == 0 else 0, tile)],
            dst_ref=rows_in.at[half + side],
            send_sem=halo_send.at[side], recv_sem=halo_recv.at[side],
            device_id=beside(side), device_id_type=MESH,
        )

    def swap(p):
        return pltpu.make_async_remote_copy(
            src_ref=x_ref.at[:, cuts[p]], dst_ref=x_far.at[:, cuts[p]],
            send_sem=swap_send.at[p], recv_sem=swap_recv.at[p],
            device_id=partner, device_id_type=MESH,
        )

    def push_row(i):
        return pltpu.make_async_remote_copy(
            src_ref=rows_out.at[i], dst_ref=rows_in.at[i], send_sem=row_send,
            recv_sem=row_recv, device_id=asker(i), device_id_type=MESH,
        )

    def push_far(p, i):
        return pltpu.make_async_remote_copy(
            src_ref=far_out.at[p, i], dst_ref=far_in.at[p, i], send_sem=far_send.at[p],
            recv_sem=far_recv.at[p], device_id=asker(i), device_id_type=MESH,
        )

    @pl.loop(1, half)
    def _(i):
        ask(i).start()

    for p in range(pieces):
        swap(p).start()
    push_halo(0).start()
    push_halo(1).start()
    want_in[0] = want_out[0]
    mates = pl.ds(1, half - 1)
    pltpu.make_async_copy(want_in.at[mates], want_in.at[mates], want_recv).wait()

    shape = (half, tile, own)
    token = lax.broadcasted_iota(jnp.int32, shape, 1)
    lane = lax.broadcasted_iota(jnp.int32, shape, 2)

    def hot(far):
        picked = lane == want_in[:, far, 0:1, :] * tile + token
        return jnp.where(picked, 1.0, 0.0).reshape(half * tile, own)

    near_hot = hot(0).astype(jnp.bfloat16)
    for p in range(pieces):
        rows_out[0:half, :, cuts[p]] = (
            dot(near_hot, x_ref[:, cuts[p]], NN).astype(jnp.bfloat16).reshape(half, tile, wide)
        )

    @pl.loop(1, half)
    def _(i):
        push_row(i).start()

    rows_in[0] = rows_out[0]

    def pick_far(p):
        far_hot = hot(1).astype(jnp.bfloat16)
        swap(p).wait_recv()
        far_out[p] = (
            dot(far_hot, x_far[:, cuts[p]], NN).astype(jnp.bfloat16).reshape(half, tile, wide)
        )

        @pl.loop(1, half)
        def _(i):
            push_far(p, i).start()

        far_in[p, 0] = far_out[p, 0]

    choose[:, : half * tile] = hot(0).T.astype(jnp.bfloat16)
    choose[:, half * tile : count * tile] = hot(1).T.astype(jnp.bfloat16)
    edge_row = lax.broadcasted_iota(jnp.int32, (own, 2 * tile), 0)
    edge_lane = lax.broadcasted_iota(jnp.int32, (own, 2 * tile), 1)
    edge_spot = jnp.where(edge_lane < tile, edge_lane, edge_lane + (frames - 2) * tile)
    choose[:, count * tile : (count + 2) * tile] = jnp.where(
        edge_row == edge_spot, 1.0, 0.0
    ).astype(jnp.bfloat16)

    for i in range(count):
        at = jnp.int32(0)
        for e in range(entries):
            at = jnp.where(slots[e] == i, e, at)
        place[i] = at

    loads[0].wait()

    @pl.loop(0, pieces)
    def _(p):
        lanes = pl.ds(pl.multiple_of(p * wide, wide), wide)
        q_ref[:, lanes] = dot(x_ref[...], weights[0, :, lanes], NN).astype(jnp.bfloat16)

    pick_far(0)
    load_cot.wait()
    loads[1].wait()

    @pl.loop(0, pieces)
    def _(p):
        lanes = pl.ds(pl.multiple_of(p * wide, wide), wide)
        g_ref[:, lanes] = dot(cot_ref[...], weights[1, lanes, :], NT).astype(jnp.bfloat16)

    push_halo(0).wait_recv()
    push_halo(1).wait_recv()
    loads[2].wait()
    loads[3].wait()

    @pl.loop(0, pieces)
    def _(p):
        lanes = pl.ds(pl.multiple_of(p * wide, wide), wide)
        ext = jnp.concatenate([rows_in[half], x_ref[...], rows_in[half + 1]], axis=0)
        k_ext[:, lanes] = dot(ext, weights[2, :, lanes], NN).astype(jnp.bfloat16)
        v_ext[:, lanes] = dot(ext, weights[3, :, lanes], NN).astype(jnp.bfloat16)

    for p in range(1, pieces):
        pick_far(p)

    mates_rows = rows_in.at[mates]
    pltpu.make_async_copy(mates_rows, mates_rows, row_recv).wait()

    @pl.loop(0, pieces)
    def _(p):
        lanes = pl.ds(pl.multiple_of(p * wide, wide), wide)
        flat = rows_in[0:half].reshape(half * tile, width)
        for weight, mem_ref in ((2, k_mem), (3, v_mem)):
            mem_ref[0:half, :, lanes] = (
                dot(flat, weights[weight, :, lanes], NN)
                .astype(jnp.bfloat16)
                .reshape(half, tile, wide)
            )

    for piece in range(pieces):
        came = far_in.at[piece, mates]
        pltpu.make_async_copy(came, came, far_recv.at[piece]).wait()

        @pl.loop(0, pieces)
        def _(p):
            lanes = pl.ds(pl.multiple_of(p * wide, wide), wide)
            flat = far_in[piece].reshape(half * tile, wide)
            for kv, mem_ref in enumerate((k_mem, v_mem)):
                part = dot(flat, weights[2 + kv, cuts[piece], lanes], NN)
                if piece > 0:
                    part += far_sum[kv, :, lanes]
                if piece < pieces - 1:
                    far_sum[kv, :, lanes] = part
                else:
                    mem_ref[half:count, :, lanes] = part.astype(jnp.bfloat16).reshape(
                        half, tile, wide
                    )

    rows = GROUP * tile
    own_head = (
        lax.broadcasted_iota(jnp.int32, (rows, cols), 0) // tile
        == lax.broadcasted_iota(jnp.int32, (rows, cols), 1) // head_dim
    )
    head_at = lax.broadcasted_iota(jnp.int32, (tile, cols), 1) // head_dim

    def spread(block):
        tall = jnp.concatenate([block] * GROUP, axis=0)
        return jnp.where(own_head, tall, jnp.zeros_like(tall))

    def fold(tall):
        flat = tall[0:tile]
        for part in range(1, GROUP):
            flat = jnp.where(head_at == part, tall[part * tile : (part + 1) * tile], flat)
        return flat

    def hide(f):
        frame = me * frames + f
        lower = (frame >= 1) & (tiles[0, f] == 1)
        upper = (frame < frames * count - 1) & (tiles[1, f] == 1)
        kept = [lower, None, upper] + [recalled[f] > j for j in range(mem)]
        return [None if k is None else jnp.where(k, 0.0, -1e30) for k in kept]

    def gather(f, lanes, ext, far):
        near = slice(f * tile, (f + 3) * tile)
        return jnp.concatenate(
            [ext[near, lanes]] + [far[spots[f * mem + j], :, lanes] for j in range(mem)],
            axis=0,
        )

    def attend(g):
        lanes = pl.ds(pl.multiple_of(g * cols, cols), cols)
        kept_at = pl.ds(pl.multiple_of(g * rows, rows), rows)
        held = [None, None]
        late = [None, None]
        for f in range(frames):
            here = slice(f * tile, (f + 1) * tile)
            keys = gather(f, lanes, k_ext, k_mem)
            values = gather(f, lanes, v_ext, v_mem)
            queries = spread(q_ref[here, lanes] * scale)
            grads = spread(g_ref[here, lanes])
            scores = dot(keys, queries, NT)
            scores = jnp.concatenate(
                [
                    part if bias is None else part + bias
                    for bias, part in zip(hide(f), jnp.split(scores, 3 + mem, axis=0))
                ],
                axis=0,
            )
            expo = jnp.exp(scores - jnp.max(scores, axis=0, keepdims=True))
            prob = expo * (1.0 / jnp.sum(expo, axis=0, keepdims=True))
            low = prob.astype(jnp.bfloat16)
            prob_grad = dot(values, grads, NT)
            delta = jnp.sum(prob * prob_grad, axis=0, keepdims=True)
            score_grad = (prob * (prob_grad - delta)).astype(jnp.bfloat16)
            kept[0, f, :, kept_at] = low
            kept[1, f, :, kept_at] = score_grad
            parts = (
                dot(score_grad, queries, NN).astype(jnp.bfloat16),
                dot(low, grads, NN).astype(jnp.bfloat16),
            )
            for kv, part in enumerate(parts):
                before = part[0:tile]
                middle = part[tile : 2 * tile].astype(jnp.float32)
                after = part[2 * tile : 3 * tile]
                if f == 0:
                    blocks[entries + 1, kv, :, lanes] = before
                else:
                    back = slice((f - 1) * tile, f * tile)
                    sums[kv, back, lanes] = (held[kv] + before.astype(jnp.float32)).astype(
                        jnp.bfloat16
                    )
                    middle = middle + late[kv]
                if f == frames - 1:
                    blocks[entries, kv, :, lanes] = after
                    sums[kv, here, lanes] = middle.astype(jnp.bfloat16)
                held[kv] = middle
                late[kv] = after.astype(jnp.float32)
                for j in range(mem):
                    blocks[f * mem + j, kv, :, lanes] = part[(3 + j) * tile : (4 + j) * tile]

    @pl.loop(0, steps)
    def _(g):
        attend(g)

    def finish(g):
        lanes = pl.ds(pl.multiple_of(g * cols, cols), cols)
        kept_at = pl.ds(pl.multiple_of(g * rows, rows), rows)
        for f in range(frames):
            here = slice(f * tile, (f + 1) * tile)
            keys = gather(f, lanes, k_ext, k_mem)
            values = gather(f, lanes, v_ext, v_mem)
            mixed[here, lanes] = fold(dot(kept[0, f, :, kept_at], values, TN)).astype(
                jnp.bfloat16
            )
            query_grad[here, lanes] = (
                fold(dot(kept[1, f, :, kept_at], keys, TN)) * scale
            ).astype(jnp.bfloat16)

    def push_near(i):
        return pltpu.make_async_remote_copy(
            src_ref=rows_out.at[i], dst_ref=near_in.at[i], send_sem=near_send,
            recv_sem=near_recv, device_id=mate(i), device_id_type=MESH,
        )

    def push_back(p, i):
        return pltpu.make_async_remote_copy(
            src_ref=far_out.at[p, i], dst_ref=back_in.at[p, i], send_sem=back_send.at[p],
            recv_sem=back_recv.at[p], device_id=mate(i), device_id_type=MESH,
        )

    def relay(p):
        return pltpu.make_async_remote_copy(
            src_ref=relay_out.at[p], dst_ref=relay_in.at[p], send_sem=relay_send.at[p],
            recv_sem=relay_recv.at[p], device_id=partner, device_id_type=MESH,
        )

    def push_edge(side):
        return pltpu.make_async_remote_copy(
            src_ref=rows_out.at[half + side], dst_ref=near_in.at[half + side],
            send_sem=edge_send.at[side], recv_sem=edge_recv.at[side],
            device_id=beside(side), device_id_type=MESH,
        )

    def collect(start, extra):
        for n in range(half + extra):
            source = place[start + n] if n < half else entries + n - half
            for kv in range(2):
                gathered[kv, n * tile : (n + 1) * tile, :] = blocks[source, kv]

    def weigh(p, slots_here):
        taken = slots_here * tile
        sent = dot(gathered[0, :taken], weights[2, cuts[p], :], NT)
        sent += dot(gathered[1, :taken], weights[3, cuts[p], :], NT)
        return sent.astype(jnp.bfloat16).reshape(slots_here, tile, wide)

    collect(half, 0)
    for p in range(pieces):
        gone = far_out.at[p, mates]
        pltpu.make_async_copy(gone, gone, far_send.at[p]).wait()
        far_out[p] = weigh(p, half)

        @pl.loop(1, half)
        def _(i):
            push_back(p, i).start()

        back_in[p, 0] = far_out[p, 0]

    collect(0, 2)
    gone = rows_out.at[mates]
    pltpu.make_async_copy(gone, gone, row_send).wait()
    for p in range(pieces):
        rows_out[:, :, cuts[p]] = weigh(p, half + 2)

    for p in range(pieces):
        came = back_in.at[p, mates]
        pltpu.make_async_copy(came, came, back_recv.at[p]).wait()
        relay_out[p] = dot(
            choose[:, half * tile : count * tile], back_in[p].reshape(half * tile, wide), NN
        ).astype(jnp.bfloat16)
        relay(p).start()
        if p == 0:

            @pl.loop(1, half)
            def _(i):
                push_near(i).start()

            push_edge(0).start()
            push_edge(1).start()
            near_in[0] = rows_out[0]

    @pl.loop(0, steps)
    def _(g):
        finish(g)

    for p in range(pieces):
        lanes = cuts[p]
        layer_ref[:, lanes] = dot(mixed[...], weights[1, :, lanes], NN).astype(jnp.bfloat16)
        total[:, lanes] = (
            dot(query_grad[...], weights[0, lanes, :], NT)
            + dot(sums[0], weights[2, lanes, :], NT)
            + dot(sums[1], weights[3, lanes, :], NT)
        )

    came = near_in.at[mates]
    pltpu.make_async_copy(came, came, near_recv).wait()
    push_edge(0).wait_recv()
    push_edge(1).wait_recv()
    for p in range(pieces):
        lanes = cuts[p]
        total[:, lanes] += dot(
            choose[:, : half * tile], near_in[0:half, :, lanes].reshape(half * tile, wide), NN
        ) + dot(
            choose[:, count * tile :],
            near_in[half : half + 2, :, lanes].reshape(2 * tile, wide),
            NN,
        )
    for p in range(pieces):
        relay(p).wait_recv()
        grad_ref[:, cuts[p]] = (total[:, cuts[p]] + relay_in[p].astype(jnp.float32)).astype(
            jnp.bfloat16
        )

    asked_of = want_out.at[mates]
    pltpu.make_async_copy(asked_of, asked_of, want_send).wait()
    gone = rows_out.at[mates]
    pltpu.make_async_copy(gone, gone, near_send).wait()
    for p in range(pieces):
        gone = far_out.at[p, mates]
        pltpu.make_async_copy(gone, gone, back_send.at[p]).wait()
        swap(p).wait_send()
        relay(p).wait_send()
    push_halo(0).wait_send()
    push_halo(1).wait_send()
    push_edge(0).wait_send()
    push_edge(1).wait_send()


def hand_over(layer_in, grad_in, layer_ref, grad_ref):
    layer_ref[...] = layer_in[...]
    grad_ref[...] = grad_in[...]


def on_device(
    latents, w_query, w_key, w_value, w_out, cotangent, memory_ids, memory_count, tile_mask
):
    frames, tile, width = latents.shape
    count = lax.axis_size("tm")
    rows = latents.reshape(-1, width)
    mem = memory_ids.shape[1]
    inner = w_query.shape[1]
    head_dim = inner // HEADS
    cols = GROUP * head_dim
    steps = inner // cols
    own = frames * tile
    half = count // 2
    wide = 2 * cols
    pieces = width // wide

    vmem = pl.BlockSpec(memory_space=pltpu.VMEM)
    smem = pl.BlockSpec(memory_space=pltpu.SMEM)
    hbm = pl.BlockSpec(memory_space=pl.ANY)
    layer_out, latent_grad = pl.pallas_call(
        functools.partial(layer_kernel, count, frames, mem, tile, head_dim, steps),
        in_specs=[smem] * 3 + [vmem] + [hbm] * 5,
        out_specs=[vmem, vmem],
        out_shape=[
            jax.ShapeDtypeStruct((own, width), jnp.bfloat16),
            jax.ShapeDtypeStruct((own, width), jnp.bfloat16),
        ],
        scratch_shapes=[
            pltpu.VMEM((4, width, inner), jnp.bfloat16),
            pltpu.VMEM((own, width), jnp.bfloat16),
            pltpu.VMEM((own, inner), jnp.bfloat16),
            pltpu.VMEM((own, inner), jnp.bfloat16),
            pltpu.VMEM((own + 2 * tile, inner), jnp.bfloat16),
            pltpu.VMEM((own + 2 * tile, inner), jnp.bfloat16),
            pltpu.VMEM((count, tile, inner), jnp.bfloat16),
            pltpu.VMEM((count, tile, inner), jnp.bfloat16),
            pltpu.VMEM((half, 2, 8, own), jnp.int32),
            pltpu.VMEM((half, 2, 8, own), jnp.int32),
            pltpu.VMEM((own, (count + 2) * tile), jnp.bfloat16),
            pltpu.VMEM((half + 2, tile, width), jnp.bfloat16),
            pltpu.VMEM((half + 2, tile, width), jnp.bfloat16),
            pltpu.VMEM((pieces, half, tile, wide), jnp.bfloat16),
            pltpu.VMEM((pieces, half, tile, wide), jnp.bfloat16),
            pltpu.VMEM((own, width), jnp.bfloat16),
            pltpu.VMEM((2, half * tile, inner), jnp.float32),
            pltpu.VMEM((2, frames, (3 + mem) * tile, steps * GROUP * tile), jnp.bfloat16),
            pltpu.VMEM((own, inner), jnp.bfloat16),
            pltpu.VMEM((own, inner), jnp.bfloat16),
            pltpu.VMEM((2, own, inner), jnp.bfloat16),
            pltpu.VMEM((frames * mem + 2, 2, tile, inner), jnp.bfloat16),
            pltpu.VMEM((2, (half + 2) * tile, inner), jnp.bfloat16),
            pltpu.VMEM((half + 2, tile, width), jnp.bfloat16),
            pltpu.VMEM((pieces, half, tile, wide), jnp.bfloat16),
            pltpu.VMEM((pieces, own, wide), jnp.bfloat16),
            pltpu.VMEM((pieces, own, wide), jnp.bfloat16),
            pltpu.VMEM((own, width), jnp.float32),
            pltpu.SMEM((frames * mem,), jnp.int32),
            pltpu.SMEM((count,), jnp.int32),
            pltpu.SemaphoreType.DMA((4,)),
            pltpu.SemaphoreType.DMA,
            pltpu.SemaphoreType.DMA,
            pltpu.SemaphoreType.DMA,
            pltpu.SemaphoreType.DMA,
            pltpu.SemaphoreType.DMA,
            pltpu.SemaphoreType.DMA((pieces,)),
            pltpu.SemaphoreType.DMA((pieces,)),
            pltpu.SemaphoreType.DMA((2,)),
            pltpu.SemaphoreType.DMA((2,)),
            pltpu.SemaphoreType.DMA,
            pltpu.SemaphoreType.DMA,
            pltpu.SemaphoreType.DMA((pieces,)),
            pltpu.SemaphoreType.DMA((pieces,)),
            pltpu.SemaphoreType.DMA((2,)),
            pltpu.SemaphoreType.DMA((2,)),
            pltpu.SemaphoreType.DMA((pieces,)),
            pltpu.SemaphoreType.DMA((pieces,)),
            pltpu.SemaphoreType.DMA((pieces,)),
            pltpu.SemaphoreType.DMA((pieces,)),
        ],
        compiler_params=pltpu.CompilerParams(
            collective_id=0, has_side_effects=True, vmem_limit_bytes=58 * 2**20
        ),
    )(
        memory_ids, memory_count, tile_mask.T, rows, cotangent.reshape(-1, width),
        w_query, w_out, w_key, w_value,
    )
    layer_out, latent_grad = pl.pallas_call(
        hand_over,
        in_specs=[vmem, vmem],
        out_specs=[vmem, vmem],
        out_shape=[jax.ShapeDtypeStruct((own, width), jnp.bfloat16)] * 2,
    )(layer_out, latent_grad)
    return (
        layer_out.reshape(frames, tile, width),
        latent_grad.reshape(frames, tile, width),
    )


def solution(mesh):
    placed = (
        P(("shard", "tm"), None, None),
        P(),
        P(),
        P(),
        P(),
        P(("shard", "tm"), None, None),
        P(("shard", "tm"), None),
        P(("shard", "tm")),
        P(("shard", "tm"), None),
    )
    return jax.shard_map(
        on_device,
        mesh=mesh,
        in_specs=placed,
        out_specs=(P(("shard", "tm"), None, None), P(("shard", "tm"), None, None)),
        check_vma=False,
    )
```

```python
import functools
import math

import jax
import jax.numpy as jnp
from jax import lax
from jax.experimental import pallas as pl
from jax.experimental.pallas import tpu as pltpu
from jax.sharding import PartitionSpec as P

HEADS = 24
GROUP = 4
NT = (((1,), (1,)), ((), ()))
NN = (((1,), (0,)), ((), ()))
TN = (((0,), (0,)), ((), ()))
MESH = pl.DeviceIdType.MESH


def dot(a, b, dims):
    return lax.dot_general(a, b, dims, preferred_element_type=jnp.float32)


def layer_kernel(
    count, frames, mem, tile, head_dim, steps,
    ids, recalled, tiles, x_ref, cot_hbm, wq_hbm, wo_hbm, wk_hbm, wv_hbm,
    layer_ref, grad_ref,
    weights, cot_ref, q_ref, g_ref, k_ext, v_ext, k_mem, v_mem, want_out, want_in, choose,
    rows_out, rows_in, far_out, far_in, x_far, far_sum, kept, mixed, query_grad, sums, blocks,
    gathered, near_in, back_in, relay_out, relay_in, total,
    spots, place,
    weight_sem, cot_sem, want_send, want_recv, row_send, row_recv, far_send, far_recv,
    halo_send, halo_recv, near_send, near_recv, back_send, back_recv, edge_send, edge_recv,
    swap_send, swap_recv, relay_send, relay_recv,
):
    me = lax.axis_index("tm")
    width = x_ref.shape[1]
    own = x_ref.shape[0]
    cols = q_ref.shape[1] // steps
    wide = 2 * cols
    half = count // 2
    pieces = width // wide
    cuts = [slice(p * wide, (p + 1) * wide) for p in range(pieces)]
    place_in = lax.rem(me, half)
    base = me - place_in
    entries = frames * mem
    scale = 1.0 / math.sqrt(head_dim)
    loads = [
        pltpu.make_async_copy(source, weights.at[i], weight_sem.at[i])
        for i, source in enumerate((wq_hbm, wo_hbm, wk_hbm, wv_hbm))
    ]
    load_cot = pltpu.make_async_copy(cot_hbm, cot_ref, cot_sem)
    loads[0].start()
    load_cot.start()
    for load in loads[1:]:
        load.start()

    def mate(i):
        return {"tm": base + lax.rem(place_in + i, half)}

    def asker(i):
        return {"tm": base + lax.rem(place_in + half - i, half)}

    partner = {"tm": lax.rem(me + half, count)}

    def beside(side):
        return {"tm": lax.rem(me + (1 if side == 0 else count - 1), count)}

    has_next = me < count - 1
    has_last = me > 0
    barrier = pltpu.get_barrier_semaphore()

    @pl.loop(1, count)
    def _(i):
        pl.semaphore_signal(
            barrier, inc=1, device_id={"tm": lax.rem(me + i, count)}, device_id_type=MESH
        )

    slots = []
    slot_at = lax.broadcasted_iota(jnp.int32, want_out.shape, 0)
    slot_at += half * lax.broadcasted_iota(jnp.int32, want_out.shape, 1)
    asked = jnp.full(want_out.shape, -frames, jnp.int32)
    for e in range(entries):
        frame = ids[e // mem, e % mem]
        owner = lax.div(frame, frames)
        away = lax.rem(owner - place_in + count, half)
        same = (owner >= base) & (owner < base + half)
        slot = away + jnp.where(same, 0, half)
        spots[e] = slot
        slots.append(slot)
        asked = jnp.where(slot_at == slot, lax.rem(frame, frames), asked)
    want_out[...] = asked

    pl.semaphore_wait(barrier, count - 1)

    def ask(i):
        return pltpu.make_async_remote_copy(
            src_ref=want_out.at[i], dst_ref=want_in.at[i], send_sem=want_send,
            recv_sem=want_recv, device_id=mate(i), device_id_type=MESH,
        )

    def push_halo(side):
        return pltpu.make_async_remote_copy(
            src_ref=x_ref.at[pl.ds((frames - 1) * tile if side == 0 else 0, tile)],
            dst_ref=rows_in.at[half + side],
            send_sem=halo_send.at[side], recv_sem=halo_recv.at[side],
            device_id=beside(side), device_id_type=MESH,
        )

    def swap(p):
        return pltpu.make_async_remote_copy(
            src_ref=x_ref.at[:, cuts[p]], dst_ref=x_far.at[:, cuts[p]],
            send_sem=swap_send.at[p], recv_sem=swap_recv.at[p],
            device_id=partner, device_id_type=MESH,
        )

    def push_row(i):
        return pltpu.make_async_remote_copy(
            src_ref=rows_out.at[i], dst_ref=rows_in.at[i], send_sem=row_send,
            recv_sem=row_recv, device_id=asker(i), device_id_type=MESH,
        )

    def push_far(p, i):
        return pltpu.make_async_remote_copy(
            src_ref=far_out.at[p, i], dst_ref=far_in.at[p, i], send_sem=far_send.at[p],
            recv_sem=far_recv.at[p], device_id=asker(i), device_id_type=MESH,
        )

    @pl.loop(1, half)
    def _(i):
        ask(i).start()

    for p in range(pieces):
        swap(p).start()
    @pl.when(has_next)
    def _():
        push_halo(0).start()

    @pl.when(has_last)
    def _():
        push_halo(1).start()

    want_in[0] = want_out[0]
    mates = pl.ds(1, half - 1)
    pltpu.make_async_copy(want_in.at[mates], want_in.at[mates], want_recv).wait()

    shape = (half, tile, own)
    token = lax.broadcasted_iota(jnp.int32, shape, 1)
    lane = lax.broadcasted_iota(jnp.int32, shape, 2)

    def hot(far):
        picked = lane == want_in[:, far, 0:1, :] * tile + token
        return jnp.where(picked, 1.0, 0.0).reshape(half * tile, own)

    near_hot = hot(0).astype(jnp.bfloat16)
    for p in range(pieces):
        rows_out[0:half, :, cuts[p]] = (
            dot(near_hot, x_ref[:, cuts[p]], NN).astype(jnp.bfloat16).reshape(half, tile, wide)
        )

    @pl.loop(1, half)
    def _(i):
        push_row(i).start()

    rows_in[0] = rows_out[0]

    def pick_far(p):
        far_hot = hot(1).astype(jnp.bfloat16)
        swap(p).wait_recv()
        far_out[p] = (
            dot(far_hot, x_far[:, cuts[p]], NN).astype(jnp.bfloat16).reshape(half, tile, wide)
        )

        @pl.loop(1, half)
        def _(i):
            push_far(p, i).start()

        far_in[p, 0] = far_out[p, 0]

    choose[:, : half * tile] = hot(0).T.astype(jnp.bfloat16)
    choose[:, half * tile : count * tile] = hot(1).T.astype(jnp.bfloat16)
    edge_row = lax.broadcasted_iota(jnp.int32, (own, 2 * tile), 0)
    edge_lane = lax.broadcasted_iota(jnp.int32, (own, 2 * tile), 1)
    edge_spot = jnp.where(edge_lane < tile, edge_lane, edge_lane + (frames - 2) * tile)
    choose[:, count * tile : (count + 2) * tile] = jnp.where(
        edge_row == edge_spot, 1.0, 0.0
    ).astype(jnp.bfloat16)

    for i in range(count):
        at = jnp.int32(0)
        for e in range(entries):
            at = jnp.where(slots[e] == i, e, at)
        place[i] = at

    loads[0].wait()

    @pl.loop(0, pieces)
    def _(p):
        lanes = pl.ds(pl.multiple_of(p * wide, wide), wide)
        q_ref[:, lanes] = dot(x_ref[...], weights[0, :, lanes], NN).astype(jnp.bfloat16)

    pick_far(0)
    load_cot.wait()
    loads[1].wait()

    @pl.loop(0, pieces)
    def _(p):
        lanes = pl.ds(pl.multiple_of(p * wide, wide), wide)
        g_ref[:, lanes] = dot(cot_ref[...], weights[1, lanes, :], NT).astype(jnp.bfloat16)

    for p in range(1, pieces):
        pick_far(p)

    loads[2].wait()
    loads[3].wait()
    mates_rows = rows_in.at[mates]
    pltpu.make_async_copy(mates_rows, mates_rows, row_recv).wait()

    @pl.loop(0, pieces)
    def _(p):
        lanes = pl.ds(pl.multiple_of(p * wide, wide), wide)
        flat = rows_in[0:half].reshape(half * tile, width)
        for weight, mem_ref in ((2, k_mem), (3, v_mem)):
            mem_ref[0:half, :, lanes] = (
                dot(flat, weights[weight, :, lanes], NN)
                .astype(jnp.bfloat16)
                .reshape(half, tile, wide)
            )

    @pl.when(has_last)
    def _():
        push_halo(0).wait_recv()

    @pl.when(has_next)
    def _():
        push_halo(1).wait_recv()

    @pl.when(jnp.logical_not(has_last))
    def _():
        rows_in[half] = jnp.zeros((tile, width), rows_in.dtype)

    @pl.when(jnp.logical_not(has_next))
    def _():
        rows_in[half + 1] = jnp.zeros((tile, width), rows_in.dtype)


    @pl.loop(0, pieces)
    def _(p):
        lanes = pl.ds(pl.multiple_of(p * wide, wide), wide)
        ext = jnp.concatenate([rows_in[half], x_ref[...], rows_in[half + 1]], axis=0)
        k_ext[:, lanes] = dot(ext, weights[2, :, lanes], NN).astype(jnp.bfloat16)
        v_ext[:, lanes] = dot(ext, weights[3, :, lanes], NN).astype(jnp.bfloat16)

    for piece in range(pieces):
        came = far_in.at[piece, mates]
        pltpu.make_async_copy(came, came, far_recv.at[piece]).wait()

        @pl.loop(0, pieces)
        def _(p):
            lanes = pl.ds(pl.multiple_of(p * wide, wide), wide)
            flat = far_in[piece].reshape(half * tile, wide)
            for kv, mem_ref in enumerate((k_mem, v_mem)):
                part = dot(flat, weights[2 + kv, cuts[piece], lanes], NN)
                if piece > 0:
                    part += far_sum[kv, :, lanes]
                if piece < pieces - 1:
                    far_sum[kv, :, lanes] = part
                else:
                    mem_ref[half:count, :, lanes] = part.astype(jnp.bfloat16).reshape(
                        half, tile, wide
                    )

    rows = GROUP * tile
    own_head = (
        lax.broadcasted_iota(jnp.int32, (rows, cols), 0) // tile
        == lax.broadcasted_iota(jnp.int32, (rows, cols), 1) // head_dim
    )
    head_at = lax.broadcasted_iota(jnp.int32, (tile, cols), 1) // head_dim

    def spread(block):
        tall = jnp.concatenate([block] * GROUP, axis=0)
        return jnp.where(own_head, tall, jnp.zeros_like(tall))

    def fold(tall):
        flat = tall[0:tile]
        for part in range(1, GROUP):
            flat = jnp.where(head_at == part, tall[part * tile : (part + 1) * tile], flat)
        return flat

    def hide(f):
        frame = me * frames + f
        lower = (frame >= 1) & (tiles[0, f] == 1)
        upper = (frame < frames * count - 1) & (tiles[1, f] == 1)
        kept = [lower, None, upper] + [recalled[f] > j for j in range(mem)]
        return [None if k is None else jnp.where(k, 0.0, -1e30) for k in kept]

    def gather(f, lanes, ext, far):
        near = slice(f * tile, (f + 3) * tile)
        return jnp.concatenate(
            [ext[near, lanes]] + [far[spots[f * mem + j], :, lanes] for j in range(mem)],
            axis=0,
        )

    def attend(g):
        lanes = pl.ds(pl.multiple_of(g * cols, cols), cols)
        kept_at = pl.ds(pl.multiple_of(g * rows, rows), rows)
        held = [None, None]
        late = [None, None]
        keys = [gather(f, lanes, k_ext, k_mem) for f in range(frames)]
        values = [gather(f, lanes, v_ext, v_mem) for f in range(frames)]
        heres = [slice(f * tile, (f + 1) * tile) for f in range(frames)]
        queries = [spread(q_ref[here, lanes] * scale) for here in heres]
        grads = [spread(g_ref[here, lanes]) for here in heres]
        raw = {}
        prob_grads = {}
        lows = {}
        score_grads = {}

        def multiply(f):
            raw[f] = dot(keys[f], queries[f], NT)
            prob_grads[f] = dot(values[f], grads[f], NT)

        def soften(f):
            scores = jnp.concatenate(
                [
                    part if bias is None else part + bias
                    for bias, part in zip(hide(f), jnp.split(raw[f], 3 + mem, axis=0))
                ],
                axis=0,
            )
            expo = jnp.exp(scores - jnp.max(scores, axis=0, keepdims=True))
            prob = expo * (1.0 / jnp.sum(expo, axis=0, keepdims=True))
            lows[f] = prob.astype(jnp.bfloat16)
            delta = jnp.sum(prob * prob_grads[f], axis=0, keepdims=True)
            score_grads[f] = (prob * (prob_grads[f] - delta)).astype(jnp.bfloat16)
            kept[0, f, :, kept_at] = lows[f]
            kept[1, f, :, kept_at] = score_grads[f]

        def spill(f):
            here = heres[f]
            parts = (
                dot(score_grads[f], queries[f], NN).astype(jnp.bfloat16),
                dot(lows[f], grads[f], NN).astype(jnp.bfloat16),
            )
            for kv, part in enumerate(parts):
                before = part[0:tile]
                middle = part[tile : 2 * tile].astype(jnp.float32)
                after = part[2 * tile : 3 * tile]
                if f == 0:
                    blocks[entries + 1, kv, :, lanes] = before
                else:
                    back = slice((f - 1) * tile, f * tile)
                    sums[kv, back, lanes] = (held[kv] + before.astype(jnp.float32)).astype(
                        jnp.bfloat16
                    )
                    middle = middle + late[kv]
                if f == frames - 1:
                    blocks[entries, kv, :, lanes] = after
                    sums[kv, here, lanes] = middle.astype(jnp.bfloat16)
                held[kv] = middle
                late[kv] = after.astype(jnp.float32)
                for j in range(mem):
                    blocks[f * mem + j, kv, :, lanes] = part[(3 + j) * tile : (4 + j) * tile]

        multiply(0)
        for f in range(frames):
            if f + 1 < frames:
                multiply(f + 1)
            soften(f)
            if f > 0:
                spill(f - 1)
        spill(frames - 1)

    @pl.loop(0, steps)
    def _(g):
        attend(g)

    def finish(g):
        lanes = pl.ds(pl.multiple_of(g * cols, cols), cols)
        kept_at = pl.ds(pl.multiple_of(g * rows, rows), rows)
        for f in range(frames):
            here = slice(f * tile, (f + 1) * tile)
            keys = gather(f, lanes, k_ext, k_mem)
            values = gather(f, lanes, v_ext, v_mem)
            mixed[here, lanes] = fold(dot(kept[0, f, :, kept_at], values, TN)).astype(
                jnp.bfloat16
            )
            query_grad[here, lanes] = (
                fold(dot(kept[1, f, :, kept_at], keys, TN)) * scale
            ).astype(jnp.bfloat16)

    def push_near(i):
        return pltpu.make_async_remote_copy(
            src_ref=rows_out.at[i], dst_ref=near_in.at[i], send_sem=near_send,
            recv_sem=near_recv, device_id=mate(i), device_id_type=MESH,
        )

    def push_back(p, i):
        return pltpu.make_async_remote_copy(
            src_ref=far_out.at[p, i], dst_ref=back_in.at[p, i], send_sem=back_send.at[p],
            recv_sem=back_recv.at[p], device_id=mate(i), device_id_type=MESH,
        )

    def relay(p):
        return pltpu.make_async_remote_copy(
            src_ref=relay_out.at[p], dst_ref=relay_in.at[p], send_sem=relay_send.at[p],
            recv_sem=relay_recv.at[p], device_id=partner, device_id_type=MESH,
        )

    def push_edge(side):
        return pltpu.make_async_remote_copy(
            src_ref=rows_out.at[half + side], dst_ref=near_in.at[half + side],
            send_sem=edge_send.at[side], recv_sem=edge_recv.at[side],
            device_id=beside(side), device_id_type=MESH,
        )

    def collect(start, extra):
        for n in range(half + extra):
            source = place[start + n] if n < half else entries + n - half
            for kv in range(2):
                gathered[kv, n * tile : (n + 1) * tile, :] = blocks[source, kv]

    def weigh(p, slots_here):
        taken = slots_here * tile
        sent = dot(gathered[0, :taken], weights[2, cuts[p], :], NT)
        sent += dot(gathered[1, :taken], weights[3, cuts[p], :], NT)
        return sent.astype(jnp.bfloat16).reshape(slots_here, tile, wide)

    collect(half, 0)
    for p in range(pieces):
        gone = far_out.at[p, mates]
        pltpu.make_async_copy(gone, gone, far_send.at[p]).wait()
        far_out[p] = weigh(p, half)

        @pl.loop(1, half)
        def _(i):
            push_back(p, i).start()

        back_in[p, 0] = far_out[p, 0]

    collect(0, 2)
    gone = rows_out.at[mates]
    pltpu.make_async_copy(gone, gone, row_send).wait()
    for p in range(pieces):
        rows_out[:, :, cuts[p]] = weigh(p, half + 2)

    for p in range(pieces):
        came = back_in.at[p, mates]
        pltpu.make_async_copy(came, came, back_recv.at[p]).wait()
        relay_out[p] = dot(
            choose[:, half * tile : count * tile], back_in[p].reshape(half * tile, wide), NN
        ).astype(jnp.bfloat16)
        relay(p).start()
        if p == 0:

            @pl.loop(1, half)
            def _(i):
                push_near(i).start()


            @pl.when(has_next)
            def _():
                push_edge(0).start()

            @pl.when(has_last)
            def _():
                push_edge(1).start()

            near_in[0] = rows_out[0]

    @pl.loop(0, steps)
    def _(g):
        finish(g)

    for p in range(pieces):
        lanes = cuts[p]
        layer_ref[:, lanes] = dot(mixed[...], weights[1, :, lanes], NN).astype(jnp.bfloat16)
        total[:, lanes] = (
            dot(query_grad[...], weights[0, lanes, :], NT)
            + dot(sums[0], weights[2, lanes, :], NT)
            + dot(sums[1], weights[3, lanes, :], NT)
        )

    came = near_in.at[mates]
    pltpu.make_async_copy(came, came, near_recv).wait()

    @pl.when(has_last)
    def _():
        push_edge(0).wait_recv()

    @pl.when(has_next)
    def _():
        push_edge(1).wait_recv()

    @pl.when(jnp.logical_not(has_last))
    def _():
        near_in[half] = jnp.zeros((tile, width), near_in.dtype)

    @pl.when(jnp.logical_not(has_next))
    def _():
        near_in[half + 1] = jnp.zeros((tile, width), near_in.dtype)

    for p in range(pieces):
        lanes = cuts[p]
        total[:, lanes] += dot(
            choose[:, : half * tile], near_in[0:half, :, lanes].reshape(half * tile, wide), NN
        ) + dot(
            choose[:, count * tile :],
            near_in[half : half + 2, :, lanes].reshape(2 * tile, wide),
            NN,
        )
    for p in range(pieces):
        relay(p).wait_recv()
        grad_ref[:, cuts[p]] = (total[:, cuts[p]] + relay_in[p].astype(jnp.float32)).astype(
            jnp.bfloat16
        )

    asked_of = want_out.at[mates]
    pltpu.make_async_copy(asked_of, asked_of, want_send).wait()
    gone = rows_out.at[mates]
    pltpu.make_async_copy(gone, gone, near_send).wait()
    for p in range(pieces):
        gone = far_out.at[p, mates]
        pltpu.make_async_copy(gone, gone, back_send.at[p]).wait()
        swap(p).wait_send()
        relay(p).wait_send()

    @pl.when(has_next)
    def _():
        push_halo(0).wait_send()
        push_edge(0).wait_send()

    @pl.when(has_last)
    def _():
        push_halo(1).wait_send()
        push_edge(1).wait_send()


def hand_over(layer_in, grad_in, layer_ref, grad_ref):
    layer_ref[...] = layer_in[...]
    grad_ref[...] = grad_in[...]


def on_device(
    latents, w_query, w_key, w_value, w_out, cotangent, memory_ids, memory_count, tile_mask
):
    frames, tile, width = latents.shape
    count = lax.axis_size("tm")
    rows = latents.reshape(-1, width)
    mem = memory_ids.shape[1]
    inner = w_query.shape[1]
    head_dim = inner // HEADS
    cols = GROUP * head_dim
    steps = inner // cols
    own = frames * tile
    half = count // 2
    wide = 2 * cols
    pieces = width // wide

    vmem = pl.BlockSpec(memory_space=pltpu.VMEM)
    smem = pl.BlockSpec(memory_space=pltpu.SMEM)
    hbm = pl.BlockSpec(memory_space=pl.ANY)
    layer_out, latent_grad = pl.pallas_call(
        functools.partial(layer_kernel, count, frames, mem, tile, head_dim, steps),
        in_specs=[smem] * 3 + [vmem] + [hbm] * 5,
        out_specs=[vmem, vmem],
        out_shape=[
            jax.ShapeDtypeStruct((own, width), jnp.bfloat16),
            jax.ShapeDtypeStruct((own, width), jnp.bfloat16),
        ],
        scratch_shapes=[
            pltpu.VMEM((4, width, inner), jnp.bfloat16),
            pltpu.VMEM((own, width), jnp.bfloat16),
            pltpu.VMEM((own, inner), jnp.bfloat16),
            pltpu.VMEM((own, inner), jnp.bfloat16),
            pltpu.VMEM((own + 2 * tile, inner), jnp.bfloat16),
            pltpu.VMEM((own + 2 * tile, inner), jnp.bfloat16),
            pltpu.VMEM((count, tile, inner), jnp.bfloat16),
            pltpu.VMEM((count, tile, inner), jnp.bfloat16),
            pltpu.VMEM((half, 2, 8, own), jnp.int32),
            pltpu.VMEM((half, 2, 8, own), jnp.int32),
            pltpu.VMEM((own, (count + 2) * tile), jnp.bfloat16),
            pltpu.VMEM((half + 2, tile, width), jnp.bfloat16),
            pltpu.VMEM((half + 2, tile, width), jnp.bfloat16),
            pltpu.VMEM((pieces, half, tile, wide), jnp.bfloat16),
            pltpu.VMEM((pieces, half, tile, wide), jnp.bfloat16),
            pltpu.VMEM((own, width), jnp.bfloat16),
            pltpu.VMEM((2, half * tile, inner), jnp.float32),
            pltpu.VMEM((2, frames, (3 + mem) * tile, steps * GROUP * tile), jnp.bfloat16),
            pltpu.VMEM((own, inner), jnp.bfloat16),
            pltpu.VMEM((own, inner), jnp.bfloat16),
            pltpu.VMEM((2, own, inner), jnp.bfloat16),
            pltpu.VMEM((frames * mem + 2, 2, tile, inner), jnp.bfloat16),
            pltpu.VMEM((2, (half + 2) * tile, inner), jnp.bfloat16),
            pltpu.VMEM((half + 2, tile, width), jnp.bfloat16),
            pltpu.VMEM((pieces, half, tile, wide), jnp.bfloat16),
            pltpu.VMEM((pieces, own, wide), jnp.bfloat16),
            pltpu.VMEM((pieces, own, wide), jnp.bfloat16),
            pltpu.VMEM((own, width), jnp.float32),
            pltpu.SMEM((frames * mem,), jnp.int32),
            pltpu.SMEM((count,), jnp.int32),
            pltpu.SemaphoreType.DMA((4,)),
            pltpu.SemaphoreType.DMA,
            pltpu.SemaphoreType.DMA,
            pltpu.SemaphoreType.DMA,
            pltpu.SemaphoreType.DMA,
            pltpu.SemaphoreType.DMA,
            pltpu.SemaphoreType.DMA((pieces,)),
            pltpu.SemaphoreType.DMA((pieces,)),
            pltpu.SemaphoreType.DMA((2,)),
            pltpu.SemaphoreType.DMA((2,)),
            pltpu.SemaphoreType.DMA,
            pltpu.SemaphoreType.DMA,
            pltpu.SemaphoreType.DMA((pieces,)),
            pltpu.SemaphoreType.DMA((pieces,)),
            pltpu.SemaphoreType.DMA((2,)),
            pltpu.SemaphoreType.DMA((2,)),
            pltpu.SemaphoreType.DMA((pieces,)),
            pltpu.SemaphoreType.DMA((pieces,)),
            pltpu.SemaphoreType.DMA((pieces,)),
            pltpu.SemaphoreType.DMA((pieces,)),
        ],
        compiler_params=pltpu.CompilerParams(
            collective_id=0, has_side_effects=True, vmem_limit_bytes=58 * 2**20
        ),
    )(
        memory_ids, memory_count, tile_mask.T, rows, cotangent.reshape(-1, width),
        w_query, w_out, w_key, w_value,
    )
    layer_out, latent_grad = pl.pallas_call(
        hand_over,
        in_specs=[vmem, vmem],
        out_specs=[vmem, vmem],
        out_shape=[jax.ShapeDtypeStruct((own, width), jnp.bfloat16)] * 2,
    )(layer_out, latent_grad)
    return (
        layer_out.reshape(frames, tile, width),
        latent_grad.reshape(frames, tile, width),
    )


def solution(mesh):
    placed = (
        P(("shard", "tm"), None, None),
        P(),
        P(),
        P(),
        P(),
        P(("shard", "tm"), None, None),
        P(("shard", "tm"), None),
        P(("shard", "tm")),
        P(("shard", "tm"), None),
    )
    return jax.shard_map(
        on_device,
        mesh=mesh,
        in_specs=placed,
        out_specs=(P(("shard", "tm"), None, None), P(("shard", "tm"), None, None)),
        check_vma=False,
    )
```

```python
import functools
import math

import jax
import jax.numpy as jnp
from jax import lax
from jax.experimental import pallas as pl
from jax.experimental.pallas import tpu as pltpu
from jax.sharding import PartitionSpec as P

HEADS = 24
GROUP = 4
NT = (((1,), (1,)), ((), ()))
NN = (((1,), (0,)), ((), ()))
TN = (((0,), (0,)), ((), ()))
MESH = pl.DeviceIdType.MESH


def dot(a, b, dims):
    return lax.dot_general(a, b, dims, preferred_element_type=jnp.float32)


def layer_kernel(
    count, frames, mem, tile, head_dim, steps,
    ids, recalled, tiles, x_ref, cot_hbm, wq_hbm, wo_hbm, wk_hbm, wv_hbm,
    layer_ref, grad_ref,
    weights, cot_ref, q_ref, g_ref, k_ext, v_ext, k_mem, v_mem, want_out, want_in, choose,
    rows_out, rows_in, far_out, far_in, x_far, far_sum, kept, mixed, query_grad, sums, blocks,
    gathered, near_in, back_in, relay_out, relay_in, total,
    spots, place,
    weight_sem, cot_sem, want_send, want_recv, row_send, row_recv, far_send, far_recv,
    halo_send, halo_recv, near_send, near_recv, back_send, back_recv, edge_send, edge_recv,
    swap_send, swap_recv, relay_send, relay_recv,
):
    me = lax.axis_index("tm")
    width = x_ref.shape[1]
    own = x_ref.shape[0]
    cols = q_ref.shape[1] // steps
    wide = 2 * cols
    half = count // 2
    pieces = width // wide
    cuts = [slice(p * wide, (p + 1) * wide) for p in range(pieces)]
    place_in = lax.rem(me, half)
    base = me - place_in
    entries = frames * mem
    scale = 1.0 / math.sqrt(head_dim)
    loads = [
        pltpu.make_async_copy(source, weights.at[i], weight_sem.at[i])
        for i, source in enumerate((wq_hbm, wo_hbm, wk_hbm, wv_hbm))
    ]
    load_cot = pltpu.make_async_copy(cot_hbm, cot_ref, cot_sem)
    loads[0].start()
    load_cot.start()
    for load in loads[1:]:
        load.start()

    def mate(i):
        return {"tm": base + lax.rem(place_in + i, half)}

    def asker(i):
        return {"tm": base + lax.rem(place_in + half - i, half)}

    partner = {"tm": lax.rem(me + half, count)}

    def beside(side):
        return {"tm": lax.rem(me + (1 if side == 0 else count - 1), count)}

    has_next = me < count - 1
    has_last = me > 0
    barrier = pltpu.get_barrier_semaphore()

    @pl.loop(1, count)
    def _(i):
        pl.semaphore_signal(
            barrier, inc=1, device_id={"tm": lax.rem(me + i, count)}, device_id_type=MESH
        )

    slots = []
    slot_at = lax.broadcasted_iota(jnp.int32, want_out.shape, 0)
    slot_at += half * lax.broadcasted_iota(jnp.int32, want_out.shape, 1)
    asked = jnp.full(want_out.shape, -frames, jnp.int32)
    for e in range(entries):
        frame = ids[e // mem, e % mem]
        owner = lax.div(frame, frames)
        away = lax.rem(owner - place_in + count, half)
        same = (owner >= base) & (owner < base + half)
        slot = away + jnp.where(same, 0, half)
        spots[e] = slot
        slots.append(slot)
        asked = jnp.where(slot_at == slot, lax.rem(frame, frames), asked)
    want_out[...] = asked

    pl.semaphore_wait(barrier, count - 1)

    def ask(i):
        return pltpu.make_async_remote_copy(
            src_ref=want_out.at[i], dst_ref=want_in.at[i], send_sem=want_send,
            recv_sem=want_recv, device_id=mate(i), device_id_type=MESH,
        )

    def push_halo(side):
        return pltpu.make_async_remote_copy(
            src_ref=x_ref.at[pl.ds((frames - 1) * tile if side == 0 else 0, tile)],
            dst_ref=rows_in.at[half + side],
            send_sem=halo_send.at[side], recv_sem=halo_recv.at[side],
            device_id=beside(side), device_id_type=MESH,
        )

    def swap(p):
        return pltpu.make_async_remote_copy(
            src_ref=x_ref.at[:, cuts[p]], dst_ref=x_far.at[:, cuts[p]],
            send_sem=swap_send.at[p], recv_sem=swap_recv.at[p],
            device_id=partner, device_id_type=MESH,
        )

    def push_row(i):
        return pltpu.make_async_remote_copy(
            src_ref=rows_out.at[i], dst_ref=rows_in.at[i], send_sem=row_send,
            recv_sem=row_recv, device_id=asker(i), device_id_type=MESH,
        )

    def push_far(p, i):
        return pltpu.make_async_remote_copy(
            src_ref=far_out.at[p, i], dst_ref=far_in.at[p, i], send_sem=far_send.at[p],
            recv_sem=far_recv.at[p], device_id=asker(i), device_id_type=MESH,
        )

    @pl.loop(1, half)
    def _(i):
        ask(i).start()

    for p in range(pieces):
        swap(p).start()
    @pl.when(has_next)
    def _():
        push_halo(0).start()

    @pl.when(has_last)
    def _():
        push_halo(1).start()

    want_in[0] = want_out[0]
    mates = pl.ds(1, half - 1)
    pltpu.make_async_copy(want_in.at[mates], want_in.at[mates], want_recv).wait()

    shape = (half, tile, own)
    token = lax.broadcasted_iota(jnp.int32, shape, 1)
    lane = lax.broadcasted_iota(jnp.int32, shape, 2)

    def hot(far):
        picked = lane == want_in[:, far, 0:1, :] * tile + token
        return jnp.where(picked, 1.0, 0.0).reshape(half * tile, own)

    near_hot = hot(0).astype(jnp.bfloat16)
    for p in range(pieces):
        rows_out[0:half, :, cuts[p]] = (
            dot(near_hot, x_ref[:, cuts[p]], NN).astype(jnp.bfloat16).reshape(half, tile, wide)
        )

    @pl.loop(1, half)
    def _(i):
        push_row(i).start()

    rows_in[0] = rows_out[0]

    def pick_far(p):
        far_hot = hot(1).astype(jnp.bfloat16)
        swap(p).wait_recv()
        far_out[p] = (
            dot(far_hot, x_far[:, cuts[p]], NN).astype(jnp.bfloat16).reshape(half, tile, wide)
        )

        @pl.loop(1, half)
        def _(i):
            push_far(p, i).start()

        far_in[p, 0] = far_out[p, 0]

    choose[:, : half * tile] = hot(0).T.astype(jnp.bfloat16)
    choose[:, half * tile : count * tile] = hot(1).T.astype(jnp.bfloat16)
    edge_row = lax.broadcasted_iota(jnp.int32, (own, 2 * tile), 0)
    edge_lane = lax.broadcasted_iota(jnp.int32, (own, 2 * tile), 1)
    edge_spot = jnp.where(edge_lane < tile, edge_lane, edge_lane + (frames - 2) * tile)
    choose[:, count * tile : (count + 2) * tile] = jnp.where(
        edge_row == edge_spot, 1.0, 0.0
    ).astype(jnp.bfloat16)

    for i in range(count):
        at = jnp.int32(0)
        for e in range(entries):
            at = jnp.where(slots[e] == i, e, at)
        place[i] = at

    loads[0].wait()

    @pl.loop(0, pieces)
    def _(p):
        lanes = pl.ds(pl.multiple_of(p * wide, wide), wide)
        q_ref[:, lanes] = dot(x_ref[...], weights[0, :, lanes], NN).astype(jnp.bfloat16)

    pick_far(0)
    load_cot.wait()
    loads[1].wait()

    @pl.loop(0, pieces)
    def _(p):
        lanes = pl.ds(pl.multiple_of(p * wide, wide), wide)
        g_ref[:, lanes] = dot(cot_ref[...], weights[1, lanes, :], NT).astype(jnp.bfloat16)

    for p in range(1, pieces):
        pick_far(p)

    loads[2].wait()
    loads[3].wait()
    mates_rows = rows_in.at[mates]
    pltpu.make_async_copy(mates_rows, mates_rows, row_recv).wait()

    @pl.loop(0, pieces)
    def _(p):
        lanes = pl.ds(pl.multiple_of(p * wide, wide), wide)
        flat = rows_in[0:half].reshape(half * tile, width)
        for weight, mem_ref in ((2, k_mem), (3, v_mem)):
            mem_ref[0:half, :, lanes] = (
                dot(flat, weights[weight, :, lanes], NN)
                .astype(jnp.bfloat16)
                .reshape(half, tile, wide)
            )

    @pl.when(has_last)
    def _():
        push_halo(0).wait_recv()

    @pl.when(has_next)
    def _():
        push_halo(1).wait_recv()

    @pl.when(jnp.logical_not(has_last))
    def _():
        rows_in[half] = jnp.zeros((tile, width), rows_in.dtype)

    @pl.when(jnp.logical_not(has_next))
    def _():
        rows_in[half + 1] = jnp.zeros((tile, width), rows_in.dtype)


    @pl.loop(0, pieces)
    def _(p):
        lanes = pl.ds(pl.multiple_of(p * wide, wide), wide)
        ext = jnp.concatenate([rows_in[half], x_ref[...], rows_in[half + 1]], axis=0)
        k_ext[:, lanes] = dot(ext, weights[2, :, lanes], NN).astype(jnp.bfloat16)
        v_ext[:, lanes] = dot(ext, weights[3, :, lanes], NN).astype(jnp.bfloat16)

    for piece in range(pieces):
        came = far_in.at[piece, mates]
        pltpu.make_async_copy(came, came, far_recv.at[piece]).wait()

        @pl.loop(0, pieces)
        def _(p):
            lanes = pl.ds(pl.multiple_of(p * wide, wide), wide)
            flat = far_in[piece].reshape(half * tile, wide)
            for kv, mem_ref in enumerate((k_mem, v_mem)):
                part = dot(flat, weights[2 + kv, cuts[piece], lanes], NN)
                if piece > 0:
                    part += far_sum[kv, :, lanes]
                if piece < pieces - 1:
                    far_sum[kv, :, lanes] = part
                else:
                    mem_ref[half:count, :, lanes] = part.astype(jnp.bfloat16).reshape(
                        half, tile, wide
                    )

    rows = GROUP * tile
    own_head = (
        lax.broadcasted_iota(jnp.int32, (rows, cols), 0) // tile
        == lax.broadcasted_iota(jnp.int32, (rows, cols), 1) // head_dim
    )
    head_at = lax.broadcasted_iota(jnp.int32, (tile, cols), 1) // head_dim

    def spread(block):
        tall = jnp.concatenate([block] * GROUP, axis=0)
        return jnp.where(own_head, tall, jnp.zeros_like(tall))

    def fold(tall):
        flat = tall[0:tile]
        for part in range(1, GROUP):
            flat = jnp.where(head_at == part, tall[part * tile : (part + 1) * tile], flat)
        return flat

    def hide(f):
        frame = me * frames + f
        lower = (frame >= 1) & (tiles[0, f] == 1)
        upper = (frame < frames * count - 1) & (tiles[1, f] == 1)
        kept = [lower, None, upper] + [recalled[f] > j for j in range(mem)]
        return [None if k is None else jnp.where(k, 0.0, -1e30) for k in kept]

    def gather(f, lanes, ext, far):
        near = slice(f * tile, (f + 3) * tile)
        return jnp.concatenate(
            [ext[near, lanes]] + [far[spots[f * mem + j], :, lanes] for j in range(mem)],
            axis=0,
        )

    def attend(g):
        lanes = pl.ds(pl.multiple_of(g * cols, cols), cols)
        kept_at = pl.ds(pl.multiple_of(g * rows, rows), rows)
        held = [None, None]
        late = [None, None]
        keys = [gather(f, lanes, k_ext, k_mem) for f in range(frames)]
        values = [gather(f, lanes, v_ext, v_mem) for f in range(frames)]
        heres = [slice(f * tile, (f + 1) * tile) for f in range(frames)]
        queries = [spread(q_ref[here, lanes] * scale) for here in heres]
        grads = [spread(g_ref[here, lanes]) for here in heres]
        raw = {}
        prob_grads = {}
        lows = {}
        score_grads = {}

        def multiply(f):
            raw[f] = dot(keys[f], queries[f], NT)
            prob_grads[f] = dot(values[f], grads[f], NT)

        def soften(f):
            scores = jnp.concatenate(
                [
                    part if bias is None else part + bias
                    for bias, part in zip(hide(f), jnp.split(raw[f], 3 + mem, axis=0))
                ],
                axis=0,
            )
            expo = jnp.exp(scores - jnp.max(scores, axis=0, keepdims=True))
            prob = expo * (1.0 / jnp.sum(expo, axis=0, keepdims=True))
            lows[f] = prob.astype(jnp.bfloat16)
            delta = jnp.sum(prob * prob_grads[f], axis=0, keepdims=True)
            score_grads[f] = (prob * (prob_grads[f] - delta)).astype(jnp.bfloat16)
            kept[0, f, :, kept_at] = lows[f]
            kept[1, f, :, kept_at] = score_grads[f]

        def spill(f):
            here = heres[f]
            parts = (
                dot(score_grads[f], queries[f], NN).astype(jnp.bfloat16),
                dot(lows[f], grads[f], NN).astype(jnp.bfloat16),
            )
            for kv, part in enumerate(parts):
                before = part[0:tile]
                middle = part[tile : 2 * tile].astype(jnp.float32)
                after = part[2 * tile : 3 * tile]
                if f == 0:
                    blocks[entries + 1, kv, :, lanes] = before
                else:
                    back = slice((f - 1) * tile, f * tile)
                    sums[kv, back, lanes] = (held[kv] + before.astype(jnp.float32)).astype(
                        jnp.bfloat16
                    )
                    middle = middle + late[kv]
                if f == frames - 1:
                    blocks[entries, kv, :, lanes] = after
                    sums[kv, here, lanes] = middle.astype(jnp.bfloat16)
                held[kv] = middle
                late[kv] = after.astype(jnp.float32)
                for j in range(mem):
                    blocks[f * mem + j, kv, :, lanes] = part[(3 + j) * tile : (4 + j) * tile]

        multiply(0)
        for f in range(frames):
            if f + 1 < frames:
                multiply(f + 1)
            soften(f)
            if f > 0:
                spill(f - 1)
        spill(frames - 1)

    @pl.loop(0, steps)
    def _(g):
        attend(g)

    def finish(g):
        lanes = pl.ds(pl.multiple_of(g * cols, cols), cols)
        kept_at = pl.ds(pl.multiple_of(g * rows, rows), rows)
        for f in range(frames):
            here = slice(f * tile, (f + 1) * tile)
            keys = gather(f, lanes, k_ext, k_mem)
            values = gather(f, lanes, v_ext, v_mem)
            mixed[here, lanes] = fold(dot(kept[0, f, :, kept_at], values, TN)).astype(
                jnp.bfloat16
            )
            query_grad[here, lanes] = (
                fold(dot(kept[1, f, :, kept_at], keys, TN)) * scale
            ).astype(jnp.bfloat16)

    def push_near(i):
        return pltpu.make_async_remote_copy(
            src_ref=rows_out.at[i], dst_ref=near_in.at[i], send_sem=near_send,
            recv_sem=near_recv, device_id=mate(i), device_id_type=MESH,
        )

    def push_back(p, i):
        return pltpu.make_async_remote_copy(
            src_ref=far_out.at[p, i], dst_ref=back_in.at[p, i], send_sem=back_send.at[p],
            recv_sem=back_recv.at[p], device_id=mate(i), device_id_type=MESH,
        )

    def relay(p):
        return pltpu.make_async_remote_copy(
            src_ref=relay_out.at[p], dst_ref=relay_in.at[p], send_sem=relay_send.at[p],
            recv_sem=relay_recv.at[p], device_id=partner, device_id_type=MESH,
        )

    def push_edge(side):
        return pltpu.make_async_remote_copy(
            src_ref=rows_out.at[half + side], dst_ref=near_in.at[half + side],
            send_sem=edge_send.at[side], recv_sem=edge_recv.at[side],
            device_id=beside(side), device_id_type=MESH,
        )

    def collect(start, extra):
        for n in range(half + extra):
            source = place[start + n] if n < half else entries + n - half
            for kv in range(2):
                gathered[kv, n * tile : (n + 1) * tile, :] = blocks[source, kv]

    def weigh(p, slots_here):
        taken = slots_here * tile
        sent = dot(gathered[0, :taken], weights[2, cuts[p], :], NT)
        sent += dot(gathered[1, :taken], weights[3, cuts[p], :], NT)
        return sent.astype(jnp.bfloat16).reshape(slots_here, tile, wide)

    collect(half, 0)
    for p in range(pieces):
        gone = far_out.at[p, mates]
        pltpu.make_async_copy(gone, gone, far_send.at[p]).wait()
        far_out[p] = weigh(p, half)

        @pl.loop(1, half)
        def _(i):
            push_back(p, i).start()

        back_in[p, 0] = far_out[p, 0]

    collect(0, 2)
    gone = rows_out.at[mates]
    pltpu.make_async_copy(gone, gone, row_send).wait()
    for p in range(pieces):
        rows_out[:, :, cuts[p]] = weigh(p, half + 2)

    for p in range(pieces):
        came = back_in.at[p, mates]
        pltpu.make_async_copy(came, came, back_recv.at[p]).wait()
        relay_out[p] = dot(
            choose[:, half * tile : count * tile], back_in[p].reshape(half * tile, wide), NN
        ).astype(jnp.bfloat16)
        relay(p).start()
        if p == 0:

            @pl.loop(1, half)
            def _(i):
                push_near(i).start()


            @pl.when(has_next)
            def _():
                push_edge(0).start()

            @pl.when(has_last)
            def _():
                push_edge(1).start()

            near_in[0] = rows_out[0]

    @pl.loop(0, steps)
    def _(g):
        finish(g)

    for p in range(pieces):
        lanes = cuts[p]
        layer_ref[:, lanes] = dot(mixed[...], weights[1, :, lanes], NN).astype(jnp.bfloat16)
        total[:, lanes] = (
            dot(query_grad[...], weights[0, lanes, :], NT)
            + dot(sums[0], weights[2, lanes, :], NT)
            + dot(sums[1], weights[3, lanes, :], NT)
        )

    came = near_in.at[mates]
    pltpu.make_async_copy(came, came, near_recv).wait()

    @pl.when(has_last)
    def _():
        push_edge(0).wait_recv()

    @pl.when(has_next)
    def _():
        push_edge(1).wait_recv()

    @pl.when(jnp.logical_not(has_last))
    def _():
        near_in[half] = jnp.zeros((tile, width), near_in.dtype)

    @pl.when(jnp.logical_not(has_next))
    def _():
        near_in[half + 1] = jnp.zeros((tile, width), near_in.dtype)

    for p in range(pieces):
        lanes = cuts[p]
        total[:, lanes] += dot(
            choose[:, : half * tile], near_in[0:half, :, lanes].reshape(half * tile, wide), NN
        ) + dot(
            choose[:, count * tile :],
            near_in[half : half + 2, :, lanes].reshape(2 * tile, wide),
            NN,
        )
    for p in range(pieces):
        relay(p).wait_recv()
        grad_ref[:, cuts[p]] = (total[:, cuts[p]] + relay_in[p].astype(jnp.float32)).astype(
            jnp.bfloat16
        )

    asked_of = want_out.at[mates]
    pltpu.make_async_copy(asked_of, asked_of, want_send).wait()
    gone = rows_out.at[mates]
    pltpu.make_async_copy(gone, gone, near_send).wait()
    for p in range(pieces):
        gone = far_out.at[p, mates]
        pltpu.make_async_copy(gone, gone, back_send.at[p]).wait()
        swap(p).wait_send()
        relay(p).wait_send()

    @pl.when(has_next)
    def _():
        push_halo(0).wait_send()
        push_edge(0).wait_send()

    @pl.when(has_last)
    def _():
        push_halo(1).wait_send()
        push_edge(1).wait_send()


def hand_over(layer_in, grad_in, layer_ref, grad_ref):
    layer_ref[...] = layer_in[...]
    grad_ref[...] = grad_in[...]


def on_device(
    latents, w_query, w_key, w_value, w_out, cotangent, memory_ids, memory_count, tile_mask
):
    frames, tile, width = latents.shape
    count = lax.axis_size("tm")
    rows = latents.reshape(-1, width)
    mem = memory_ids.shape[1]
    inner = w_query.shape[1]
    head_dim = inner // HEADS
    cols = GROUP * head_dim
    steps = inner // cols
    own = frames * tile
    half = count // 2
    wide = 2 * cols
    pieces = width // wide

    vmem = pl.BlockSpec(memory_space=pltpu.VMEM)
    smem = pl.BlockSpec(memory_space=pltpu.SMEM)
    hbm = pl.BlockSpec(memory_space=pl.ANY)
    layer_out, latent_grad = pl.pallas_call(
        functools.partial(layer_kernel, count, frames, mem, tile, head_dim, steps),
        in_specs=[smem] * 3 + [vmem] + [hbm] * 5,
        out_specs=[vmem, vmem],
        out_shape=[pltpu.VMEM((own, width), jnp.bfloat16)] * 2,
        scratch_shapes=[
            pltpu.VMEM((4, width, inner), jnp.bfloat16),
            pltpu.VMEM((own, width), jnp.bfloat16),
            pltpu.VMEM((own, inner), jnp.bfloat16),
            pltpu.VMEM((own, inner), jnp.bfloat16),
            pltpu.VMEM((own + 2 * tile, inner), jnp.bfloat16),
            pltpu.VMEM((own + 2 * tile, inner), jnp.bfloat16),
            pltpu.VMEM((count, tile, inner), jnp.bfloat16),
            pltpu.VMEM((count, tile, inner), jnp.bfloat16),
            pltpu.VMEM((half, 2, 8, own), jnp.int32),
            pltpu.VMEM((half, 2, 8, own), jnp.int32),
            pltpu.VMEM((own, (count + 2) * tile), jnp.bfloat16),
            pltpu.VMEM((half + 2, tile, width), jnp.bfloat16),
            pltpu.VMEM((half + 2, tile, width), jnp.bfloat16),
            pltpu.VMEM((pieces, half, tile, wide), jnp.bfloat16),
            pltpu.VMEM((pieces, half, tile, wide), jnp.bfloat16),
            pltpu.VMEM((own, width), jnp.bfloat16),
            pltpu.VMEM((2, half * tile, inner), jnp.float32),
            pltpu.VMEM((2, frames, (3 + mem) * tile, steps * GROUP * tile), jnp.bfloat16),
            pltpu.VMEM((own, inner), jnp.bfloat16),
            pltpu.VMEM((own, inner), jnp.bfloat16),
            pltpu.VMEM((2, own, inner), jnp.bfloat16),
            pltpu.VMEM((frames * mem + 2, 2, tile, inner), jnp.bfloat16),
            pltpu.VMEM((2, (half + 2) * tile, inner), jnp.bfloat16),
            pltpu.VMEM((half + 2, tile, width), jnp.bfloat16),
            pltpu.VMEM((pieces, half, tile, wide), jnp.bfloat16),
            pltpu.VMEM((pieces, own, wide), jnp.bfloat16),
            pltpu.VMEM((pieces, own, wide), jnp.bfloat16),
            pltpu.VMEM((own, width), jnp.float32),
            pltpu.SMEM((frames * mem,), jnp.int32),
            pltpu.SMEM((count,), jnp.int32),
            pltpu.SemaphoreType.DMA((4,)),
            pltpu.SemaphoreType.DMA,
            pltpu.SemaphoreType.DMA,
            pltpu.SemaphoreType.DMA,
            pltpu.SemaphoreType.DMA,
            pltpu.SemaphoreType.DMA,
            pltpu.SemaphoreType.DMA((pieces,)),
            pltpu.SemaphoreType.DMA((pieces,)),
            pltpu.SemaphoreType.DMA((2,)),
            pltpu.SemaphoreType.DMA((2,)),
            pltpu.SemaphoreType.DMA,
            pltpu.SemaphoreType.DMA,
            pltpu.SemaphoreType.DMA((pieces,)),
            pltpu.SemaphoreType.DMA((pieces,)),
            pltpu.SemaphoreType.DMA((2,)),
            pltpu.SemaphoreType.DMA((2,)),
            pltpu.SemaphoreType.DMA((pieces,)),
            pltpu.SemaphoreType.DMA((pieces,)),
            pltpu.SemaphoreType.DMA((pieces,)),
            pltpu.SemaphoreType.DMA((pieces,)),
        ],
        compiler_params=pltpu.CompilerParams(
            collective_id=0, has_side_effects=True, vmem_limit_bytes=58 * 2**20
        ),
    )(
        memory_ids, memory_count, tile_mask.T, rows, cotangent.reshape(-1, width),
        w_query, w_out, w_key, w_value,
    )
    layer_out, latent_grad = pl.pallas_call(
        hand_over,
        in_specs=[vmem, vmem],
        out_specs=[vmem, vmem],
        out_shape=[jax.ShapeDtypeStruct((own, width), jnp.bfloat16)] * 2,
    )(
        pltpu.with_memory_space_constraint(layer_out, pltpu.VMEM),
        pltpu.with_memory_space_constraint(latent_grad, pltpu.VMEM),
    )
    return (
        layer_out.reshape(frames, tile, width),
        latent_grad.reshape(frames, tile, width),
    )


def solution(mesh):
    placed = (
        P(("shard", "tm"), None, None),
        P(),
        P(),
        P(),
        P(),
        P(("shard", "tm"), None, None),
        P(("shard", "tm"), None),
        P(("shard", "tm")),
        P(("shard", "tm"), None),
    )
    return jax.shard_map(
        on_device,
        mesh=mesh,
        in_specs=placed,
        out_specs=(P(("shard", "tm"), None, None), P(("shard", "tm"), None, None)),
        check_vma=False,
    )
```

```python
import functools
import math

import jax
import jax.numpy as jnp
from jax import lax
from jax.experimental import pallas as pl
from jax.experimental.pallas import tpu as pltpu
from jax.sharding import PartitionSpec as P

HEADS = 24
GROUP = 4
NT = (((1,), (1,)), ((), ()))
NN = (((1,), (0,)), ((), ()))
TN = (((0,), (0,)), ((), ()))
MESH = pl.DeviceIdType.MESH


def dot(a, b, dims):
    return lax.dot_general(a, b, dims, preferred_element_type=jnp.float32)


def layer_kernel(
    count, frames, mem, tile, head_dim, steps,
    ids, recalled, tiles, x_hbm, cot_hbm, wq_hbm, wo_hbm, wk_hbm, wv_hbm,
    layer_ref, grad_ref,
    weights, x_ref, cot_ref, q_ref, g_ref, k_ext, v_ext, k_mem, v_mem, want_out, want_in, choose,
    rows_out, rows_in, far_out, far_in, x_far, far_sum, kept, mixed, query_grad, sums, blocks,
    gathered, near_in, back_in, relay_out, relay_in, total,
    spots, place,
    weight_sem, x_sem, cot_sem, want_send, want_recv, row_send, row_recv, far_send, far_recv,
    halo_send, halo_recv, near_send, near_recv, back_send, back_recv, edge_send, edge_recv,
    swap_send, swap_recv, relay_send, relay_recv,
):
    me = lax.axis_index("tm")
    width = x_ref.shape[1]
    own = x_ref.shape[0]
    cols = q_ref.shape[1] // steps
    wide = 2 * cols
    half = count // 2
    pieces = width // wide
    cuts = [slice(p * wide, (p + 1) * wide) for p in range(pieces)]
    place_in = lax.rem(me, half)
    base = me - place_in
    entries = frames * mem
    scale = 1.0 / math.sqrt(head_dim)
    loads = [
        pltpu.make_async_copy(source, weights.at[i], weight_sem.at[i])
        for i, source in enumerate((wq_hbm, wo_hbm, wk_hbm, wv_hbm))
    ]
    load_x = pltpu.make_async_copy(x_hbm, x_ref, x_sem)
    load_cot = pltpu.make_async_copy(cot_hbm, cot_ref, cot_sem)
    load_x.start()

    def mate(i):
        return {"tm": base + lax.rem(place_in + i, half)}

    def asker(i):
        return {"tm": base + lax.rem(place_in + half - i, half)}

    partner = {"tm": lax.rem(me + half, count)}

    def beside(side):
        return {"tm": lax.rem(me + (1 if side == 0 else count - 1), count)}

    has_next = me < count - 1
    has_last = me > 0
    barrier = pltpu.get_barrier_semaphore()

    @pl.loop(1, count)
    def _(i):
        pl.semaphore_signal(
            barrier, inc=1, device_id={"tm": lax.rem(me + i, count)}, device_id_type=MESH
        )

    loads[0].start()
    load_cot.start()
    for load in loads[1:]:
        load.start()

    slots = []
    slot_at = lax.broadcasted_iota(jnp.int32, want_out.shape, 0)
    slot_at += half * lax.broadcasted_iota(jnp.int32, want_out.shape, 1)
    asked = jnp.full(want_out.shape, -frames, jnp.int32)
    for e in range(entries):
        frame = ids[e // mem, e % mem]
        owner = lax.div(frame, frames)
        away = lax.rem(owner - place_in + count, half)
        same = (owner >= base) & (owner < base + half)
        slot = away + jnp.where(same, 0, half)
        spots[e] = slot
        slots.append(slot)
        asked = jnp.where(slot_at == slot, lax.rem(frame, frames), asked)
    want_out[...] = asked

    load_x.wait()
    pl.semaphore_wait(barrier, count - 1)

    def ask(i):
        return pltpu.make_async_remote_copy(
            src_ref=want_out.at[i], dst_ref=want_in.at[i], send_sem=want_send,
            recv_sem=want_recv, device_id=mate(i), device_id_type=MESH,
        )

    def push_halo(side):
        return pltpu.make_async_remote_copy(
            src_ref=x_ref.at[pl.ds((frames - 1) * tile if side == 0 else 0, tile)],
            dst_ref=rows_in.at[half + side],
            send_sem=halo_send.at[side], recv_sem=halo_recv.at[side],
            device_id=beside(side), device_id_type=MESH,
        )

    def swap(p):
        return pltpu.make_async_remote_copy(
            src_ref=x_ref.at[:, cuts[p]], dst_ref=x_far.at[:, cuts[p]],
            send_sem=swap_send.at[p], recv_sem=swap_recv.at[p],
            device_id=partner, device_id_type=MESH,
        )

    def push_row(i):
        return pltpu.make_async_remote_copy(
            src_ref=rows_out.at[i], dst_ref=rows_in.at[i], send_sem=row_send,
            recv_sem=row_recv, device_id=asker(i), device_id_type=MESH,
        )

    def push_far(p, i):
        return pltpu.make_async_remote_copy(
            src_ref=far_out.at[p, i], dst_ref=far_in.at[p, i], send_sem=far_send.at[p],
            recv_sem=far_recv.at[p], device_id=asker(i), device_id_type=MESH,
        )

    @pl.loop(1, half)
    def _(i):
        ask(i).start()

    for p in range(pieces):
        swap(p).start()
    @pl.when(has_next)
    def _():
        push_halo(0).start()

    @pl.when(has_last)
    def _():
        push_halo(1).start()

    want_in[0] = want_out[0]
    mates = pl.ds(1, half - 1)
    pltpu.make_async_copy(want_in.at[mates], want_in.at[mates], want_recv).wait()

    shape = (half, tile, own)
    token = lax.broadcasted_iota(jnp.int32, shape, 1)
    lane = lax.broadcasted_iota(jnp.int32, shape, 2)

    def hot(far):
        picked = lane == want_in[:, far, 0:1, :] * tile + token
        return jnp.where(picked, 1.0, 0.0).reshape(half * tile, own)

    near_hot = hot(0).astype(jnp.bfloat16)
    for p in range(pieces):
        rows_out[0:half, :, cuts[p]] = (
            dot(near_hot, x_ref[:, cuts[p]], NN).astype(jnp.bfloat16).reshape(half, tile, wide)
        )

    @pl.loop(1, half)
    def _(i):
        push_row(i).start()

    rows_in[0] = rows_out[0]

    def pick_far(p):
        far_hot = hot(1).astype(jnp.bfloat16)
        swap(p).wait_recv()
        far_out[p] = (
            dot(far_hot, x_far[:, cuts[p]], NN).astype(jnp.bfloat16).reshape(half, tile, wide)
        )

        @pl.loop(1, half)
        def _(i):
            push_far(p, i).start()

        far_in[p, 0] = far_out[p, 0]

    choose[:, : half * tile] = hot(0).T.astype(jnp.bfloat16)
    choose[:, half * tile : count * tile] = hot(1).T.astype(jnp.bfloat16)
    edge_row = lax.broadcasted_iota(jnp.int32, (own, 2 * tile), 0)
    edge_lane = lax.broadcasted_iota(jnp.int32, (own, 2 * tile), 1)
    edge_spot = jnp.where(edge_lane < tile, edge_lane, edge_lane + (frames - 2) * tile)
    choose[:, count * tile : (count + 2) * tile] = jnp.where(
        edge_row == edge_spot, 1.0, 0.0
    ).astype(jnp.bfloat16)

    for i in range(count):
        at = jnp.int32(0)
        for e in range(entries):
            at = jnp.where(slots[e] == i, e, at)
        place[i] = at

    loads[0].wait()

    @pl.loop(0, pieces)
    def _(p):
        lanes = pl.ds(pl.multiple_of(p * wide, wide), wide)
        q_ref[:, lanes] = dot(x_ref[...], weights[0, :, lanes], NN).astype(jnp.bfloat16)

    pick_far(0)
    load_cot.wait()
    loads[1].wait()

    @pl.loop(0, pieces)
    def _(p):
        lanes = pl.ds(pl.multiple_of(p * wide, wide), wide)
        g_ref[:, lanes] = dot(cot_ref[...], weights[1, lanes, :], NT).astype(jnp.bfloat16)

    for p in range(1, pieces):
        pick_far(p)

    loads[2].wait()
    loads[3].wait()
    mates_rows = rows_in.at[mates]
    pltpu.make_async_copy(mates_rows, mates_rows, row_recv).wait()

    @pl.loop(0, pieces)
    def _(p):
        lanes = pl.ds(pl.multiple_of(p * wide, wide), wide)
        flat = rows_in[0:half].reshape(half * tile, width)
        for weight, mem_ref in ((2, k_mem), (3, v_mem)):
            mem_ref[0:half, :, lanes] = (
                dot(flat, weights[weight, :, lanes], NN)
                .astype(jnp.bfloat16)
                .reshape(half, tile, wide)
            )

    @pl.when(has_last)
    def _():
        push_halo(0).wait_recv()

    @pl.when(has_next)
    def _():
        push_halo(1).wait_recv()

    @pl.when(jnp.logical_not(has_last))
    def _():
        rows_in[half] = jnp.zeros((tile, width), rows_in.dtype)

    @pl.when(jnp.logical_not(has_next))
    def _():
        rows_in[half + 1] = jnp.zeros((tile, width), rows_in.dtype)


    @pl.loop(0, pieces)
    def _(p):
        lanes = pl.ds(pl.multiple_of(p * wide, wide), wide)
        ext = jnp.concatenate([rows_in[half], x_ref[...], rows_in[half + 1]], axis=0)
        k_ext[:, lanes] = dot(ext, weights[2, :, lanes], NN).astype(jnp.bfloat16)
        v_ext[:, lanes] = dot(ext, weights[3, :, lanes], NN).astype(jnp.bfloat16)

    for piece in range(pieces):
        came = far_in.at[piece, mates]
        pltpu.make_async_copy(came, came, far_recv.at[piece]).wait()

        @pl.loop(0, pieces)
        def _(p):
            lanes = pl.ds(pl.multiple_of(p * wide, wide), wide)
            flat = far_in[piece].reshape(half * tile, wide)
            for kv, mem_ref in enumerate((k_mem, v_mem)):
                part = dot(flat, weights[2 + kv, cuts[piece], lanes], NN)
                if piece > 0:
                    part += far_sum[kv, :, lanes]
                if piece < pieces - 1:
                    far_sum[kv, :, lanes] = part
                else:
                    mem_ref[half:count, :, lanes] = part.astype(jnp.bfloat16).reshape(
                        half, tile, wide
                    )

    rows = GROUP * tile
    own_head = (
        lax.broadcasted_iota(jnp.int32, (rows, cols), 0) // tile
        == lax.broadcasted_iota(jnp.int32, (rows, cols), 1) // head_dim
    )
    head_at = lax.broadcasted_iota(jnp.int32, (tile, cols), 1) // head_dim

    def spread(block):
        tall = jnp.concatenate([block] * GROUP, axis=0)
        return jnp.where(own_head, tall, jnp.zeros_like(tall))

    def fold(tall):
        flat = tall[0:tile]
        for part in range(1, GROUP):
            flat = jnp.where(head_at == part, tall[part * tile : (part + 1) * tile], flat)
        return flat

    def hide(f):
        frame = me * frames + f
        lower = (frame >= 1) & (tiles[0, f] == 1)
        upper = (frame < frames * count - 1) & (tiles[1, f] == 1)
        kept = [lower, None, upper] + [recalled[f] > j for j in range(mem)]
        return [None if k is None else jnp.where(k, 0.0, -1e30) for k in kept]

    def gather(f, lanes, ext, far):
        near = slice(f * tile, (f + 3) * tile)
        return jnp.concatenate(
            [ext[near, lanes]] + [far[spots[f * mem + j], :, lanes] for j in range(mem)],
            axis=0,
        )

    def attend(g):
        lanes = pl.ds(pl.multiple_of(g * cols, cols), cols)
        kept_at = pl.ds(pl.multiple_of(g * rows, rows), rows)
        held = [None, None]
        late = [None, None]
        keys = [gather(f, lanes, k_ext, k_mem) for f in range(frames)]
        values = [gather(f, lanes, v_ext, v_mem) for f in range(frames)]
        heres = [slice(f * tile, (f + 1) * tile) for f in range(frames)]
        queries = [spread(q_ref[here, lanes] * scale) for here in heres]
        grads = [spread(g_ref[here, lanes]) for here in heres]
        raw = {}
        prob_grads = {}
        lows = {}
        score_grads = {}

        def multiply(f):
            raw[f] = dot(keys[f], queries[f], NT)
            prob_grads[f] = dot(values[f], grads[f], NT)

        def soften(f):
            scores = jnp.concatenate(
                [
                    part if bias is None else part + bias
                    for bias, part in zip(hide(f), jnp.split(raw[f], 3 + mem, axis=0))
                ],
                axis=0,
            )
            expo = jnp.exp(scores - jnp.max(scores, axis=0, keepdims=True))
            prob = expo * (1.0 / jnp.sum(expo, axis=0, keepdims=True))
            lows[f] = prob.astype(jnp.bfloat16)
            delta = jnp.sum(prob * prob_grads[f], axis=0, keepdims=True)
            score_grads[f] = (prob * (prob_grads[f] - delta)).astype(jnp.bfloat16)
            kept[0, f, :, kept_at] = lows[f]
            kept[1, f, :, kept_at] = score_grads[f]

        def spill(f):
            here = heres[f]
            parts = (
                dot(score_grads[f], queries[f], NN).astype(jnp.bfloat16),
                dot(lows[f], grads[f], NN).astype(jnp.bfloat16),
            )
            for kv, part in enumerate(parts):
                before = part[0:tile]
                middle = part[tile : 2 * tile].astype(jnp.float32)
                after = part[2 * tile : 3 * tile]
                if f == 0:
                    blocks[entries + 1, kv, :, lanes] = before
                else:
                    back = slice((f - 1) * tile, f * tile)
                    sums[kv, back, lanes] = (held[kv] + before.astype(jnp.float32)).astype(
                        jnp.bfloat16
                    )
                    middle = middle + late[kv]
                if f == frames - 1:
                    blocks[entries, kv, :, lanes] = after
                    sums[kv, here, lanes] = middle.astype(jnp.bfloat16)
                held[kv] = middle
                late[kv] = after.astype(jnp.float32)
                for j in range(mem):
                    blocks[f * mem + j, kv, :, lanes] = part[(3 + j) * tile : (4 + j) * tile]

        multiply(0)
        for f in range(frames):
            if f + 1 < frames:
                multiply(f + 1)
            soften(f)
            if f > 0:
                spill(f - 1)
        spill(frames - 1)

    @pl.loop(0, steps)
    def _(g):
        attend(g)

    def finish(g):
        lanes = pl.ds(pl.multiple_of(g * cols, cols), cols)
        kept_at = pl.ds(pl.multiple_of(g * rows, rows), rows)
        for f in range(frames):
            here = slice(f * tile, (f + 1) * tile)
            keys = gather(f, lanes, k_ext, k_mem)
            values = gather(f, lanes, v_ext, v_mem)
            mixed[here, lanes] = fold(dot(kept[0, f, :, kept_at], values, TN)).astype(
                jnp.bfloat16
            )
            query_grad[here, lanes] = (
                fold(dot(kept[1, f, :, kept_at], keys, TN)) * scale
            ).astype(jnp.bfloat16)

    def push_near(i):
        return pltpu.make_async_remote_copy(
            src_ref=rows_out.at[i], dst_ref=near_in.at[i], send_sem=near_send,
            recv_sem=near_recv, device_id=mate(i), device_id_type=MESH,
        )

    def push_back(p, i):
        return pltpu.make_async_remote_copy(
            src_ref=far_out.at[p, i], dst_ref=back_in.at[p, i], send_sem=back_send.at[p],
            recv_sem=back_recv.at[p], device_id=mate(i), device_id_type=MESH,
        )

    def relay(p):
        return pltpu.make_async_remote_copy(
            src_ref=relay_out.at[p], dst_ref=relay_in.at[p], send_sem=relay_send.at[p],
            recv_sem=relay_recv.at[p], device_id=partner, device_id_type=MESH,
        )

    def push_edge(side):
        return pltpu.make_async_remote_copy(
            src_ref=rows_out.at[half + side], dst_ref=near_in.at[half + side],
            send_sem=edge_send.at[side], recv_sem=edge_recv.at[side],
            device_id=beside(side), device_id_type=MESH,
        )

    def collect(start, extra):
        for n in range(half + extra):
            source = place[start + n] if n < half else entries + n - half
            for kv in range(2):
                gathered[kv, n * tile : (n + 1) * tile, :] = blocks[source, kv]

    def weigh(p, slots_here):
        taken = slots_here * tile
        sent = dot(gathered[0, :taken], weights[2, cuts[p], :], NT)
        sent += dot(gathered[1, :taken], weights[3, cuts[p], :], NT)
        return sent.astype(jnp.bfloat16).reshape(slots_here, tile, wide)

    collect(half, 0)
    for p in range(pieces):
        gone = far_out.at[p, mates]
        pltpu.make_async_copy(gone, gone, far_send.at[p]).wait()
        far_out[p] = weigh(p, half)

        @pl.loop(1, half)
        def _(i):
            push_back(p, i).start()

        back_in[p, 0] = far_out[p, 0]

    collect(0, 2)
    gone = rows_out.at[mates]
    pltpu.make_async_copy(gone, gone, row_send).wait()
    for p in range(pieces):
        rows_out[:, :, cuts[p]] = weigh(p, half + 2)

    for p in range(pieces):
        came = back_in.at[p, mates]
        pltpu.make_async_copy(came, came, back_recv.at[p]).wait()
        relay_out[p] = dot(
            choose[:, half * tile : count * tile], back_in[p].reshape(half * tile, wide), NN
        ).astype(jnp.bfloat16)
        relay(p).start()
        if p == 0:

            @pl.loop(1, half)
            def _(i):
                push_near(i).start()


            @pl.when(has_next)
            def _():
                push_edge(0).start()

            @pl.when(has_last)
            def _():
                push_edge(1).start()

            near_in[0] = rows_out[0]

    @pl.loop(0, steps)
    def _(g):
        finish(g)

    for p in range(pieces):
        lanes = cuts[p]
        layer_ref[:, lanes] = dot(mixed[...], weights[1, :, lanes], NN).astype(jnp.bfloat16)
        total[:, lanes] = (
            dot(query_grad[...], weights[0, lanes, :], NT)
            + dot(sums[0], weights[2, lanes, :], NT)
            + dot(sums[1], weights[3, lanes, :], NT)
        )

    came = near_in.at[mates]
    pltpu.make_async_copy(came, came, near_recv).wait()

    @pl.when(has_last)
    def _():
        push_edge(0).wait_recv()

    @pl.when(has_next)
    def _():
        push_edge(1).wait_recv()

    @pl.when(jnp.logical_not(has_last))
    def _():
        near_in[half] = jnp.zeros((tile, width), near_in.dtype)

    @pl.when(jnp.logical_not(has_next))
    def _():
        near_in[half + 1] = jnp.zeros((tile, width), near_in.dtype)

    for p in range(pieces):
        lanes = cuts[p]
        total[:, lanes] += dot(
            choose[:, : half * tile], near_in[0:half, :, lanes].reshape(half * tile, wide), NN
        ) + dot(
            choose[:, count * tile :],
            near_in[half : half + 2, :, lanes].reshape(2 * tile, wide),
            NN,
        )
    for p in range(pieces):
        relay(p).wait_recv()
        grad_ref[:, cuts[p]] = (total[:, cuts[p]] + relay_in[p].astype(jnp.float32)).astype(
            jnp.bfloat16
        )

    asked_of = want_out.at[mates]
    pltpu.make_async_copy(asked_of, asked_of, want_send).wait()
    gone = rows_out.at[mates]
    pltpu.make_async_copy(gone, gone, near_send).wait()
    for p in range(pieces):
        gone = far_out.at[p, mates]
        pltpu.make_async_copy(gone, gone, back_send.at[p]).wait()
        swap(p).wait_send()
        relay(p).wait_send()

    @pl.when(has_next)
    def _():
        push_halo(0).wait_send()
        push_edge(0).wait_send()

    @pl.when(has_last)
    def _():
        push_halo(1).wait_send()
        push_edge(1).wait_send()


def hand_over(layer_in, grad_in, layer_ref, grad_ref):
    layer_ref[...] = layer_in[...]
    grad_ref[...] = grad_in[...]


def on_device(
    latents, w_query, w_key, w_value, w_out, cotangent, memory_ids, memory_count, tile_mask
):
    frames, tile, width = latents.shape
    count = lax.axis_size("tm")
    rows = latents.reshape(-1, width)
    mem = memory_ids.shape[1]
    inner = w_query.shape[1]
    head_dim = inner // HEADS
    cols = GROUP * head_dim
    steps = inner // cols
    own = frames * tile
    half = count // 2
    wide = 2 * cols
    pieces = width // wide

    vmem = pl.BlockSpec(memory_space=pltpu.VMEM)
    smem = pl.BlockSpec(memory_space=pltpu.SMEM)
    hbm = pl.BlockSpec(memory_space=pl.ANY)
    layer_out, latent_grad = pl.pallas_call(
        functools.partial(layer_kernel, count, frames, mem, tile, head_dim, steps),
        in_specs=[smem] * 3 + [hbm] * 6,
        out_specs=[vmem, vmem],
        out_shape=[pltpu.VMEM((own, width), jnp.bfloat16)] * 2,
        scratch_shapes=[
            pltpu.VMEM((4, width, inner), jnp.bfloat16),
            pltpu.VMEM((own, width), jnp.bfloat16),
            pltpu.VMEM((own, width), jnp.bfloat16),
            pltpu.VMEM((own, inner), jnp.bfloat16),
            pltpu.VMEM((own, inner), jnp.bfloat16),
            pltpu.VMEM((own + 2 * tile, inner), jnp.bfloat16),
            pltpu.VMEM((own + 2 * tile, inner), jnp.bfloat16),
            pltpu.VMEM((count, tile, inner), jnp.bfloat16),
            pltpu.VMEM((count, tile, inner), jnp.bfloat16),
            pltpu.VMEM((half, 2, 8, own), jnp.int32),
            pltpu.VMEM((half, 2, 8, own), jnp.int32),
            pltpu.VMEM((own, (count + 2) * tile), jnp.bfloat16),
            pltpu.VMEM((half + 2, tile, width), jnp.bfloat16),
            pltpu.VMEM((half + 2, tile, width), jnp.bfloat16),
            pltpu.VMEM((pieces, half, tile, wide), jnp.bfloat16),
            pltpu.VMEM((pieces, half, tile, wide), jnp.bfloat16),
            pltpu.VMEM((own, width), jnp.bfloat16),
            pltpu.VMEM((2, half * tile, inner), jnp.float32),
            pltpu.VMEM((2, frames, (3 + mem) * tile, steps * GROUP * tile), jnp.bfloat16),
            pltpu.VMEM((own, inner), jnp.bfloat16),
            pltpu.VMEM((own, inner), jnp.bfloat16),
            pltpu.VMEM((2, own, inner), jnp.bfloat16),
            pltpu.VMEM((frames * mem + 2, 2, tile, inner), jnp.bfloat16),
            pltpu.VMEM((2, (half + 2) * tile, inner), jnp.bfloat16),
            pltpu.VMEM((half + 2, tile, width), jnp.bfloat16),
            pltpu.VMEM((pieces, half, tile, wide), jnp.bfloat16),
            pltpu.VMEM((pieces, own, wide), jnp.bfloat16),
            pltpu.VMEM((pieces, own, wide), jnp.bfloat16),
            pltpu.VMEM((own, width), jnp.float32),
            pltpu.SMEM((frames * mem,), jnp.int32),
            pltpu.SMEM((count,), jnp.int32),
            pltpu.SemaphoreType.DMA((4,)),
            pltpu.SemaphoreType.DMA,
            pltpu.SemaphoreType.DMA,
            pltpu.SemaphoreType.DMA,
            pltpu.SemaphoreType.DMA,
            pltpu.SemaphoreType.DMA,
            pltpu.SemaphoreType.DMA,
            pltpu.SemaphoreType.DMA((pieces,)),
            pltpu.SemaphoreType.DMA((pieces,)),
            pltpu.SemaphoreType.DMA((2,)),
            pltpu.SemaphoreType.DMA((2,)),
            pltpu.SemaphoreType.DMA,
            pltpu.SemaphoreType.DMA,
            pltpu.SemaphoreType.DMA((pieces,)),
            pltpu.SemaphoreType.DMA((pieces,)),
            pltpu.SemaphoreType.DMA((2,)),
            pltpu.SemaphoreType.DMA((2,)),
            pltpu.SemaphoreType.DMA((pieces,)),
            pltpu.SemaphoreType.DMA((pieces,)),
            pltpu.SemaphoreType.DMA((pieces,)),
            pltpu.SemaphoreType.DMA((pieces,)),
        ],
        compiler_params=pltpu.CompilerParams(
            collective_id=0, has_side_effects=True, vmem_limit_bytes=58 * 2**20
        ),
    )(
        memory_ids, memory_count, tile_mask.T, rows, cotangent.reshape(-1, width),
        w_query, w_out, w_key, w_value,
    )
    layer_out, latent_grad = pl.pallas_call(
        hand_over,
        in_specs=[vmem, vmem],
        out_specs=[vmem, vmem],
        out_shape=[jax.ShapeDtypeStruct((own, width), jnp.bfloat16)] * 2,
    )(
        pltpu.with_memory_space_constraint(layer_out, pltpu.VMEM),
        pltpu.with_memory_space_constraint(latent_grad, pltpu.VMEM),
    )
    return (
        layer_out.reshape(frames, tile, width),
        latent_grad.reshape(frames, tile, width),
    )


def solution(mesh):
    placed = (
        P(("shard", "tm"), None, None),
        P(),
        P(),
        P(),
        P(),
        P(("shard", "tm"), None, None),
        P(("shard", "tm"), None),
        P(("shard", "tm")),
        P(("shard", "tm"), None),
    )
    return jax.shard_map(
        on_device,
        mesh=mesh,
        in_specs=placed,
        out_specs=(P(("shard", "tm"), None, None), P(("shard", "tm"), None, None)),
        check_vma=False,
    )
```

```python
import functools
import math

import jax
import jax.numpy as jnp
from jax import lax
from jax.experimental import pallas as pl
from jax.experimental.pallas import tpu as pltpu
from jax.sharding import PartitionSpec as P

HEADS = 24
GROUP = 4
NT = (((1,), (1,)), ((), ()))
NN = (((1,), (0,)), ((), ()))
TN = (((0,), (0,)), ((), ()))
MESH = pl.DeviceIdType.MESH


def dot(a, b, dims):
    return lax.dot_general(a, b, dims, preferred_element_type=jnp.float32)


def layer_kernel(
    count, frames, mem, tile, head_dim, steps,
    ids, recalled, tiles, x_ref, cot_hbm, wq_hbm, wo_hbm, wk_hbm, wv_hbm,
    layer_ref, grad_ref,
    weights, cot_ref, q_ref, g_ref, k_ext, v_ext, k_mem, v_mem, want_out, want_in, choose,
    rows_out, rows_in, far_out, far_in, x_far, far_sum, kept, mixed, query_grad, sums, blocks,
    gathered, near_in, back_in, relay_out, relay_in, total,
    spots, place,
    weight_sem, cot_sem, want_send, want_recv, row_send, row_recv, far_send, far_recv,
    halo_send, halo_recv, near_send, near_recv, back_send, back_recv, edge_send, edge_recv,
    swap_send, swap_recv, relay_send, relay_recv,
):
    me = lax.axis_index("tm")
    width = x_ref.shape[1]
    own = x_ref.shape[0]
    cols = q_ref.shape[1] // steps
    wide = 2 * cols
    half = count // 2
    pieces = width // wide
    cuts = [slice(p * wide, (p + 1) * wide) for p in range(pieces)]
    place_in = lax.rem(me, half)
    base = me - place_in
    entries = frames * mem
    scale = 1.0 / math.sqrt(head_dim)
    loads = [
        pltpu.make_async_copy(source, weights.at[i], weight_sem.at[i])
        for i, source in enumerate((wq_hbm, wo_hbm, wk_hbm, wv_hbm))
    ]
    load_cot = pltpu.make_async_copy(cot_hbm, cot_ref, cot_sem)
    loads[0].start()
    load_cot.start()
    for load in loads[1:]:
        load.start()

    def mate(i):
        return {"tm": base + lax.rem(place_in + i, half)}

    def asker(i):
        return {"tm": base + lax.rem(place_in + half - i, half)}

    partner = {"tm": lax.rem(me + half, count)}

    def beside(side):
        return {"tm": lax.rem(me + (1 if side == 0 else count - 1), count)}

    has_next = me < count - 1
    has_last = me > 0
    barrier = pltpu.get_barrier_semaphore()

    @pl.loop(1, count)
    def _(i):
        pl.semaphore_signal(
            barrier, inc=1, device_id={"tm": lax.rem(me + i, count)}, device_id_type=MESH
        )

    slots = []
    slot_at = lax.broadcasted_iota(jnp.int32, want_out.shape, 0)
    slot_at += half * lax.broadcasted_iota(jnp.int32, want_out.shape, 1)
    asked = jnp.full(want_out.shape, -frames, jnp.int32)
    for e in range(entries):
        frame = ids[e // mem, e % mem]
        owner = lax.div(frame, frames)
        away = lax.rem(owner - place_in + count, half)
        same = (owner >= base) & (owner < base + half)
        slot = away + jnp.where(same, 0, half)
        spots[e] = slot
        slots.append(slot)
        asked = jnp.where(slot_at == slot, lax.rem(frame, frames), asked)
    want_out[...] = asked

    pl.semaphore_wait(barrier, count - 1)

    def ask(i):
        return pltpu.make_async_remote_copy(
            src_ref=want_out.at[i], dst_ref=want_in.at[i], send_sem=want_send,
            recv_sem=want_recv, device_id=mate(i), device_id_type=MESH,
        )

    def push_halo(side):
        return pltpu.make_async_remote_copy(
            src_ref=x_ref.at[pl.ds((frames - 1) * tile if side == 0 else 0, tile)],
            dst_ref=rows_in.at[half + side],
            send_sem=halo_send.at[side], recv_sem=halo_recv.at[side],
            device_id=beside(side), device_id_type=MESH,
        )

    def swap(p):
        return pltpu.make_async_remote_copy(
            src_ref=x_ref.at[:, cuts[p]], dst_ref=x_far.at[:, cuts[p]],
            send_sem=swap_send.at[p], recv_sem=swap_recv.at[p],
            device_id=partner, device_id_type=MESH,
        )

    def push_row(i):
        return pltpu.make_async_remote_copy(
            src_ref=rows_out.at[i], dst_ref=rows_in.at[i], send_sem=row_send,
            recv_sem=row_recv, device_id=asker(i), device_id_type=MESH,
        )

    def push_far(p, i):
        return pltpu.make_async_remote_copy(
            src_ref=far_out.at[p, i], dst_ref=far_in.at[p, i], send_sem=far_send.at[p],
            recv_sem=far_recv.at[p], device_id=asker(i), device_id_type=MESH,
        )

    @pl.loop(1, half)
    def _(i):
        ask(i).start()

    for p in range(pieces):
        swap(p).start()
    @pl.when(has_next)
    def _():
        push_halo(0).start()

    @pl.when(has_last)
    def _():
        push_halo(1).start()

    want_in[0] = want_out[0]
    mates = pl.ds(1, half - 1)
    pltpu.make_async_copy(want_in.at[mates], want_in.at[mates], want_recv).wait()

    shape = (half, tile, own)
    token = lax.broadcasted_iota(jnp.int32, shape, 1)
    lane = lax.broadcasted_iota(jnp.int32, shape, 2)

    def hot(far):
        picked = lane == want_in[:, far, 0:1, :] * tile + token
        return jnp.where(picked, 1.0, 0.0).reshape(half * tile, own)

    near_hot = hot(0).astype(jnp.bfloat16)
    for p in range(pieces):
        rows_out[0:half, :, cuts[p]] = (
            dot(near_hot, x_ref[:, cuts[p]], NN).astype(jnp.bfloat16).reshape(half, tile, wide)
        )

    @pl.loop(1, half)
    def _(i):
        push_row(i).start()

    rows_in[0] = rows_out[0]

    def pick_far(p):
        far_hot = hot(1).astype(jnp.bfloat16)
        swap(p).wait_recv()
        far_out[p] = (
            dot(far_hot, x_far[:, cuts[p]], NN).astype(jnp.bfloat16).reshape(half, tile, wide)
        )

        @pl.loop(1, half)
        def _(i):
            push_far(p, i).start()

        far_in[p, 0] = far_out[p, 0]

    choose[:, : half * tile] = hot(0).T.astype(jnp.bfloat16)
    choose[:, half * tile : count * tile] = hot(1).T.astype(jnp.bfloat16)
    edge_row = lax.broadcasted_iota(jnp.int32, (own, 2 * tile), 0)
    edge_lane = lax.broadcasted_iota(jnp.int32, (own, 2 * tile), 1)
    edge_spot = jnp.where(edge_lane < tile, edge_lane, edge_lane + (frames - 2) * tile)
    choose[:, count * tile : (count + 2) * tile] = jnp.where(
        edge_row == edge_spot, 1.0, 0.0
    ).astype(jnp.bfloat16)

    for i in range(count):
        at = jnp.int32(0)
        for e in range(entries):
            at = jnp.where(slots[e] == i, e, at)
        place[i] = at

    loads[0].wait()

    @pl.loop(0, pieces)
    def _(p):
        lanes = pl.ds(pl.multiple_of(p * wide, wide), wide)
        q_ref[:, lanes] = dot(x_ref[...], weights[0, :, lanes], NN).astype(jnp.bfloat16)

    pick_far(0)
    load_cot.wait()
    loads[1].wait()

    @pl.loop(0, pieces)
    def _(p):
        lanes = pl.ds(pl.multiple_of(p * wide, wide), wide)
        g_ref[:, lanes] = dot(cot_ref[...], weights[1, lanes, :], NT).astype(jnp.bfloat16)

    for p in range(1, pieces):
        pick_far(p)

    loads[2].wait()
    loads[3].wait()
    mates_rows = rows_in.at[mates]
    pltpu.make_async_copy(mates_rows, mates_rows, row_recv).wait()

    @pl.loop(0, pieces)
    def _(p):
        lanes = pl.ds(pl.multiple_of(p * wide, wide), wide)
        flat = rows_in[0:half].reshape(half * tile, width)
        for weight, mem_ref in ((2, k_mem), (3, v_mem)):
            mem_ref[0:half, :, lanes] = (
                dot(flat, weights[weight, :, lanes], NN)
                .astype(jnp.bfloat16)
                .reshape(half, tile, wide)
            )

    @pl.when(has_last)
    def _():
        push_halo(0).wait_recv()

    @pl.when(has_next)
    def _():
        push_halo(1).wait_recv()

    @pl.when(jnp.logical_not(has_last))
    def _():
        rows_in[half] = jnp.zeros((tile, width), rows_in.dtype)

    @pl.when(jnp.logical_not(has_next))
    def _():
        rows_in[half + 1] = jnp.zeros((tile, width), rows_in.dtype)


    @pl.loop(0, pieces)
    def _(p):
        lanes = pl.ds(pl.multiple_of(p * wide, wide), wide)
        ext = jnp.concatenate([rows_in[half], x_ref[...], rows_in[half + 1]], axis=0)
        k_ext[:, lanes] = dot(ext, weights[2, :, lanes], NN).astype(jnp.bfloat16)
        v_ext[:, lanes] = dot(ext, weights[3, :, lanes], NN).astype(jnp.bfloat16)

    for piece in range(pieces):
        came = far_in.at[piece, mates]
        pltpu.make_async_copy(came, came, far_recv.at[piece]).wait()

        @pl.loop(0, pieces)
        def _(p):
            lanes = pl.ds(pl.multiple_of(p * wide, wide), wide)
            flat = far_in[piece].reshape(half * tile, wide)
            for kv, mem_ref in enumerate((k_mem, v_mem)):
                part = dot(flat, weights[2 + kv, cuts[piece], lanes], NN)
                if piece > 0:
                    part += far_sum[kv, :, lanes]
                if piece < pieces - 1:
                    far_sum[kv, :, lanes] = part
                else:
                    mem_ref[half:count, :, lanes] = part.astype(jnp.bfloat16).reshape(
                        half, tile, wide
                    )

    rows = GROUP * tile
    own_head = (
        lax.broadcasted_iota(jnp.int32, (rows, cols), 0) // tile
        == lax.broadcasted_iota(jnp.int32, (rows, cols), 1) // head_dim
    )
    head_at = lax.broadcasted_iota(jnp.int32, (tile, cols), 1) // head_dim

    def spread(block):
        tall = jnp.concatenate([block] * GROUP, axis=0)
        return jnp.where(own_head, tall, jnp.zeros_like(tall))

    def fold(tall):
        flat = tall[0:tile]
        for part in range(1, GROUP):
            flat = jnp.where(head_at == part, tall[part * tile : (part + 1) * tile], flat)
        return flat

    def hide(f):
        frame = me * frames + f
        lower = (frame >= 1) & (tiles[0, f] == 1)
        upper = (frame < frames * count - 1) & (tiles[1, f] == 1)
        kept = [lower, None, upper] + [recalled[f] > j for j in range(mem)]
        return [None if k is None else jnp.where(k, 0.0, -1e30) for k in kept]

    def gather(f, lanes, ext, far):
        near = slice(f * tile, (f + 3) * tile)
        return jnp.concatenate(
            [ext[near, lanes]] + [far[spots[f * mem + j], :, lanes] for j in range(mem)],
            axis=0,
        )

    def attend(g):
        lanes = pl.ds(pl.multiple_of(g * cols, cols), cols)
        kept_at = pl.ds(pl.multiple_of(g * rows, rows), rows)
        held = [None, None]
        late = [None, None]
        keys = [gather(f, lanes, k_ext, k_mem) for f in range(frames)]
        values = [gather(f, lanes, v_ext, v_mem) for f in range(frames)]
        heres = [slice(f * tile, (f + 1) * tile) for f in range(frames)]
        queries = [spread(q_ref[here, lanes] * scale) for here in heres]
        grads = [spread(g_ref[here, lanes]) for here in heres]
        raw = {}
        prob_grads = {}
        lows = {}
        score_grads = {}

        def multiply(f):
            raw[f] = dot(keys[f], queries[f], NT)
            prob_grads[f] = dot(values[f], grads[f], NT)

        def soften(f):
            scores = jnp.concatenate(
                [
                    part if bias is None else part + bias
                    for bias, part in zip(hide(f), jnp.split(raw[f], 3 + mem, axis=0))
                ],
                axis=0,
            )
            expo = jnp.exp(scores - jnp.max(scores, axis=0, keepdims=True))
            prob = expo * (1.0 / jnp.sum(expo, axis=0, keepdims=True))
            lows[f] = prob.astype(jnp.bfloat16)
            delta = jnp.sum(prob * prob_grads[f], axis=0, keepdims=True)
            score_grads[f] = (prob * (prob_grads[f] - delta)).astype(jnp.bfloat16)
            kept[0, f, :, kept_at] = lows[f]
            kept[1, f, :, kept_at] = score_grads[f]

        def spill(f):
            here = heres[f]
            parts = (
                dot(score_grads[f], queries[f], NN).astype(jnp.bfloat16),
                dot(lows[f], grads[f], NN).astype(jnp.bfloat16),
            )
            for kv, part in enumerate(parts):
                before = part[0:tile]
                middle = part[tile : 2 * tile].astype(jnp.float32)
                after = part[2 * tile : 3 * tile]
                if f == 0:
                    blocks[entries + 1, kv, :, lanes] = before
                else:
                    back = slice((f - 1) * tile, f * tile)
                    sums[kv, back, lanes] = (held[kv] + before.astype(jnp.float32)).astype(
                        jnp.bfloat16
                    )
                    middle = middle + late[kv]
                if f == frames - 1:
                    blocks[entries, kv, :, lanes] = after
                    sums[kv, here, lanes] = middle.astype(jnp.bfloat16)
                held[kv] = middle
                late[kv] = after.astype(jnp.float32)
                for j in range(mem):
                    blocks[f * mem + j, kv, :, lanes] = part[(3 + j) * tile : (4 + j) * tile]

        multiply(0)
        multiply(1)
        for f in range(frames):
            soften(f)
            if f + 2 < frames:
                multiply(f + 2)
            if f > 0:
                spill(f - 1)
        spill(frames - 1)

    @pl.loop(0, steps)
    def _(g):
        attend(g)

    def finish(g):
        lanes = pl.ds(pl.multiple_of(g * cols, cols), cols)
        kept_at = pl.ds(pl.multiple_of(g * rows, rows), rows)
        for f in range(frames):
            here = slice(f * tile, (f + 1) * tile)
            keys = gather(f, lanes, k_ext, k_mem)
            values = gather(f, lanes, v_ext, v_mem)
            mixed[here, lanes] = fold(dot(kept[0, f, :, kept_at], values, TN)).astype(
                jnp.bfloat16
            )
            query_grad[here, lanes] = (
                fold(dot(kept[1, f, :, kept_at], keys, TN)) * scale
            ).astype(jnp.bfloat16)

    def push_near(i):
        return pltpu.make_async_remote_copy(
            src_ref=rows_out.at[i], dst_ref=near_in.at[i], send_sem=near_send,
            recv_sem=near_recv, device_id=mate(i), device_id_type=MESH,
        )

    def push_back(p, i):
        return pltpu.make_async_remote_copy(
            src_ref=far_out.at[p, i], dst_ref=back_in.at[p, i], send_sem=back_send.at[p],
            recv_sem=back_recv.at[p], device_id=mate(i), device_id_type=MESH,
        )

    def relay(p):
        return pltpu.make_async_remote_copy(
            src_ref=relay_out.at[p], dst_ref=relay_in.at[p], send_sem=relay_send.at[p],
            recv_sem=relay_recv.at[p], device_id=partner, device_id_type=MESH,
        )

    def push_edge(side):
        return pltpu.make_async_remote_copy(
            src_ref=rows_out.at[half + side], dst_ref=near_in.at[half + side],
            send_sem=edge_send.at[side], recv_sem=edge_recv.at[side],
            device_id=beside(side), device_id_type=MESH,
        )

    def collect(start, extra):
        for n in range(half + extra):
            source = place[start + n] if n < half else entries + n - half
            for kv in range(2):
                gathered[kv, n * tile : (n + 1) * tile, :] = blocks[source, kv]

    def weigh(p, slots_here):
        taken = slots_here * tile
        sent = dot(gathered[0, :taken], weights[2, cuts[p], :], NT)
        sent += dot(gathered[1, :taken], weights[3, cuts[p], :], NT)
        return sent.astype(jnp.bfloat16).reshape(slots_here, tile, wide)

    collect(half, 0)
    for p in range(pieces):
        gone = far_out.at[p, mates]
        pltpu.make_async_copy(gone, gone, far_send.at[p]).wait()
        far_out[p] = weigh(p, half)

        @pl.loop(1, half)
        def _(i):
            push_back(p, i).start()

        back_in[p, 0] = far_out[p, 0]

    collect(0, 2)
    gone = rows_out.at[mates]
    pltpu.make_async_copy(gone, gone, row_send).wait()
    for p in range(pieces):
        rows_out[:, :, cuts[p]] = weigh(p, half + 2)

    for p in range(pieces):
        came = back_in.at[p, mates]
        pltpu.make_async_copy(came, came, back_recv.at[p]).wait()
        relay_out[p] = dot(
            choose[:, half * tile : count * tile], back_in[p].reshape(half * tile, wide), NN
        ).astype(jnp.bfloat16)
        relay(p).start()
        if p == 0:

            @pl.loop(1, half)
            def _(i):
                push_near(i).start()


            @pl.when(has_next)
            def _():
                push_edge(0).start()

            @pl.when(has_last)
            def _():
                push_edge(1).start()

            near_in[0] = rows_out[0]

    @pl.loop(0, steps)
    def _(g):
        finish(g)

    for p in range(pieces):
        lanes = cuts[p]
        layer_ref[:, lanes] = dot(mixed[...], weights[1, :, lanes], NN).astype(jnp.bfloat16)
        total[:, lanes] = (
            dot(query_grad[...], weights[0, lanes, :], NT)
            + dot(sums[0], weights[2, lanes, :], NT)
            + dot(sums[1], weights[3, lanes, :], NT)
        )

    came = near_in.at[mates]
    pltpu.make_async_copy(came, came, near_recv).wait()

    @pl.when(has_last)
    def _():
        push_edge(0).wait_recv()

    @pl.when(has_next)
    def _():
        push_edge(1).wait_recv()

    @pl.when(jnp.logical_not(has_last))
    def _():
        near_in[half] = jnp.zeros((tile, width), near_in.dtype)

    @pl.when(jnp.logical_not(has_next))
    def _():
        near_in[half + 1] = jnp.zeros((tile, width), near_in.dtype)

    for p in range(pieces):
        lanes = cuts[p]
        total[:, lanes] += dot(
            choose[:, : half * tile], near_in[0:half, :, lanes].reshape(half * tile, wide), NN
        ) + dot(
            choose[:, count * tile :],
            near_in[half : half + 2, :, lanes].reshape(2 * tile, wide),
            NN,
        )
    for p in range(pieces):
        relay(p).wait_recv()
        grad_ref[:, cuts[p]] = (total[:, cuts[p]] + relay_in[p].astype(jnp.float32)).astype(
            jnp.bfloat16
        )

    asked_of = want_out.at[mates]
    pltpu.make_async_copy(asked_of, asked_of, want_send).wait()
    gone = rows_out.at[mates]
    pltpu.make_async_copy(gone, gone, near_send).wait()
    for p in range(pieces):
        gone = far_out.at[p, mates]
        pltpu.make_async_copy(gone, gone, back_send.at[p]).wait()
        swap(p).wait_send()
        relay(p).wait_send()

    @pl.when(has_next)
    def _():
        push_halo(0).wait_send()
        push_edge(0).wait_send()

    @pl.when(has_last)
    def _():
        push_halo(1).wait_send()
        push_edge(1).wait_send()


def hand_over(layer_in, grad_in, layer_ref, grad_ref):
    layer_ref[...] = layer_in[...]
    grad_ref[...] = grad_in[...]


def on_device(
    latents, w_query, w_key, w_value, w_out, cotangent, memory_ids, memory_count, tile_mask
):
    frames, tile, width = latents.shape
    count = lax.axis_size("tm")
    rows = latents.reshape(-1, width)
    mem = memory_ids.shape[1]
    inner = w_query.shape[1]
    head_dim = inner // HEADS
    cols = GROUP * head_dim
    steps = inner // cols
    own = frames * tile
    half = count // 2
    wide = 2 * cols
    pieces = width // wide

    vmem = pl.BlockSpec(memory_space=pltpu.VMEM)
    smem = pl.BlockSpec(memory_space=pltpu.SMEM)
    hbm = pl.BlockSpec(memory_space=pl.ANY)
    layer_out, latent_grad = pl.pallas_call(
        functools.partial(layer_kernel, count, frames, mem, tile, head_dim, steps),
        in_specs=[smem] * 3 + [vmem] + [hbm] * 5,
        out_specs=[vmem, vmem],
        out_shape=[pltpu.VMEM((own, width), jnp.bfloat16)] * 2,
        scratch_shapes=[
            pltpu.VMEM((4, width, inner), jnp.bfloat16),
            pltpu.VMEM((own, width), jnp.bfloat16),
            pltpu.VMEM((own, inner), jnp.bfloat16),
            pltpu.VMEM((own, inner), jnp.bfloat16),
            pltpu.VMEM((own + 2 * tile, inner), jnp.bfloat16),
            pltpu.VMEM((own + 2 * tile, inner), jnp.bfloat16),
            pltpu.VMEM((count, tile, inner), jnp.bfloat16),
            pltpu.VMEM((count, tile, inner), jnp.bfloat16),
            pltpu.VMEM((half, 2, 8, own), jnp.int32),
            pltpu.VMEM((half, 2, 8, own), jnp.int32),
            pltpu.VMEM((own, (count + 2) * tile), jnp.bfloat16),
            pltpu.VMEM((half + 2, tile, width), jnp.bfloat16),
            pltpu.VMEM((half + 2, tile, width), jnp.bfloat16),
            pltpu.VMEM((pieces, half, tile, wide), jnp.bfloat16),
            pltpu.VMEM((pieces, half, tile, wide), jnp.bfloat16),
            pltpu.VMEM((own, width), jnp.bfloat16),
            pltpu.VMEM((2, half * tile, inner), jnp.float32),
            pltpu.VMEM((2, frames, (3 + mem) * tile, steps * GROUP * tile), jnp.bfloat16),
            pltpu.VMEM((own, inner), jnp.bfloat16),
            pltpu.VMEM((own, inner), jnp.bfloat16),
            pltpu.VMEM((2, own, inner), jnp.bfloat16),
            pltpu.VMEM((frames * mem + 2, 2, tile, inner), jnp.bfloat16),
            pltpu.VMEM((2, (half + 2) * tile, inner), jnp.bfloat16),
            pltpu.VMEM((half + 2, tile, width), jnp.bfloat16),
            pltpu.VMEM((pieces, half, tile, wide), jnp.bfloat16),
            pltpu.VMEM((pieces, own, wide), jnp.bfloat16),
            pltpu.VMEM((pieces, own, wide), jnp.bfloat16),
            pltpu.VMEM((own, width), jnp.float32),
            pltpu.SMEM((frames * mem,), jnp.int32),
            pltpu.SMEM((count,), jnp.int32),
            pltpu.SemaphoreType.DMA((4,)),
            pltpu.SemaphoreType.DMA,
            pltpu.SemaphoreType.DMA,
            pltpu.SemaphoreType.DMA,
            pltpu.SemaphoreType.DMA,
            pltpu.SemaphoreType.DMA,
            pltpu.SemaphoreType.DMA((pieces,)),
            pltpu.SemaphoreType.DMA((pieces,)),
            pltpu.SemaphoreType.DMA((2,)),
            pltpu.SemaphoreType.DMA((2,)),
            pltpu.SemaphoreType.DMA,
            pltpu.SemaphoreType.DMA,
            pltpu.SemaphoreType.DMA((pieces,)),
            pltpu.SemaphoreType.DMA((pieces,)),
            pltpu.SemaphoreType.DMA((2,)),
            pltpu.SemaphoreType.DMA((2,)),
            pltpu.SemaphoreType.DMA((pieces,)),
            pltpu.SemaphoreType.DMA((pieces,)),
            pltpu.SemaphoreType.DMA((pieces,)),
            pltpu.SemaphoreType.DMA((pieces,)),
        ],
        compiler_params=pltpu.CompilerParams(
            collective_id=0, has_side_effects=True, vmem_limit_bytes=58 * 2**20
        ),
    )(
        memory_ids, memory_count, tile_mask.T, rows, cotangent.reshape(-1, width),
        w_query, w_out, w_key, w_value,
    )
    layer_out, latent_grad = pl.pallas_call(
        hand_over,
        in_specs=[vmem, vmem],
        out_specs=[vmem, vmem],
        out_shape=[jax.ShapeDtypeStruct((own, width), jnp.bfloat16)] * 2,
    )(
        pltpu.with_memory_space_constraint(layer_out, pltpu.VMEM),
        pltpu.with_memory_space_constraint(latent_grad, pltpu.VMEM),
    )
    return (
        layer_out.reshape(frames, tile, width),
        latent_grad.reshape(frames, tile, width),
    )


def solution(mesh):
    placed = (
        P(("shard", "tm"), None, None),
        P(),
        P(),
        P(),
        P(),
        P(("shard", "tm"), None, None),
        P(("shard", "tm"), None),
        P(("shard", "tm")),
        P(("shard", "tm"), None),
    )
    return jax.shard_map(
        on_device,
        mesh=mesh,
        in_specs=placed,
        out_specs=(P(("shard", "tm"), None, None), P(("shard", "tm"), None, None)),
        check_vma=False,
    )
```
